32 devices in a mesh: seq: 16 (over z, x, core), head: 2 (over y).
Axes of the slice: x: 2, y: 2, z: 4, core: 2. Of those that a mesh axis runs over, the one named last changes fastest.
Arguments:
- q_local: bfloat16 [8192, 2048], P('seq', 'head'), may hold values from -130 to 130
- k_local: bfloat16 [8192, 2048], P('seq', 'head'), may hold values from -6 to 6
- nearby_band_contents: bfloat16 [8192, 2048], P('seq', 'head'), may hold values from -6 to 6
- q_stride: bfloat16 [8192, 2048], P('seq', 'head'), may hold values from -130 to 130
- k_stride: bfloat16 [8192, 2048], P('seq', 'head'), may hold values from -6 to 6
- v_stride: bfloat16 [8192, 2048], P('seq', 'head'), may hold values from -6 to 6
- w_local: bfloat16 [2048, 4096], P('head'), may hold values from -0.09375 to 0.09375
- dilated_combiner: bfloat16 [2048, 4096], P('head'), may hold values from -0.09375 to 0.09375
Outputs:
- mixed: bfloat16 [8192, 4096], P(('seq', 'head'))
The draws below stay inside these ranges and needn't reach their ends.
All inputs are finite; a program needn't handle non-finite values.
Results may differ from the reference program's by a relative error of at most 0.0056.
Values may be sent and summed in bfloat16 or wider, within the bound.
No kernel may reach another device: no remote copies, remote signals or barrier semaphores. Data moves between devices by JAX's collectives and lax.ppermute only.
A program may use at most 128 MiB of HBM per device.

```python
import jax
import jax.numpy as jnp
from jax import lax

D = 4096
HL = 16
HS = 16
HD = 128
STRIDE = 256
BAND = 256
TOK_DEV = 512
SEQLEN = 8192


def make_pair(key, tag, heads):
    base = jax.random.fold_in(key, tag)
    first, second = jax.random.split(base, 2)
    dimension_tuple = (SEQLEN, heads, HD)
    requester_positions = jnp.clip(jax.random.normal(first, dimension_tuple, jnp.float32), -6.0, 6.0)
    keys = jnp.clip(jax.random.normal(second, dimension_tuple, jnp.float32), -6.0, 6.0)
    return (requester_positions.reshape(SEQLEN, heads * HD), keys.reshape(SEQLEN, heads * HD))


def draw_q_local(key, part):
    return make_pair(key, 11, HL)[0].astype(jnp.bfloat16)


def draw_k_local(key, part):
    return make_pair(key, 11, HL)[1].astype(jnp.bfloat16)


def draw_q_stride(key, part):
    return make_pair(key, 12, HS)[0].astype(jnp.bfloat16)


def draw_k_stride(key, part):
    return make_pair(key, 12, HS)[1].astype(jnp.bfloat16)


def block_levels(stream_key, shape, pieces, low, largest):
    def one(dim, blocks):
        steps = jax.random.uniform(jax.random.fold_in(jax.random.fold_in(stream_key, 6), dim), (blocks,), jnp.float32, low / len(pieces), largest / len(pieces))
        return jnp.repeat(jnp.exp(steps), shape[dim] // blocks).reshape((-1,) + (1,) * (len(shape) - dim - 1))

    level = one(*pieces[0])
    for cut in pieces[1:]:
        level = level * one(*cut)
    return level


def normal_values(own_key, extent, width, limit, cuts=(), held_as=jnp.bfloat16):
    loudness = block_levels(own_key, extent, cuts, -0.22, 0.18) if cuts else 1.0
    drawn = jax.random.normal(own_key, extent, jnp.float32) * width * loudness
    return jnp.minimum(jnp.maximum(drawn, -limit), limit).astype(held_as)


def setup_inputs(seed: int = 0) -> dict:
    key_list = jax.random.split(jax.random.key(seed), 9)
    q_local = draw_q_local(jax.random.fold_in(key_list[8], 71), 0)
    k_local = draw_k_local(jax.random.fold_in(key_list[8], 71), 0)
    nearby_band_contents = normal_values(key_list[2], (SEQLEN, HL * HD), 1.0, 6.0, ((0, 16), (1, 2)))
    q_stride = draw_q_stride(jax.random.fold_in(key_list[8], 71), 0)
    k_stride = draw_k_stride(jax.random.fold_in(key_list[8], 71), 0)
    v_stride = normal_values(key_list[5], (SEQLEN, HS * HD), 1.0, 6.0, ((0, 16), (1, 2)))
    w_local = normal_values(key_list[6], (HL * HD, D), D ** -0.5, 0.09375, ((0, 2),))
    dilated_combiner = normal_values(key_list[7], (HS * HD, D), D ** -0.5, 0.09375, ((0, 2),))
    return {"q_local": q_local, "k_local": k_local, "nearby_band_contents": nearby_band_contents, "q_stride": q_stride, "k_stride": k_stride, "v_stride": v_stride, "w_local": w_local, "dilated_combiner": dilated_combiner}


def attend(requester_positions, key, value_vectors, valid):
    inverse_root_depth = requester_positions.shape[-1] ** -0.5
    similarity_grid = jnp.einsum('suf,iuf->usi', requester_positions.astype(jnp.float32), key.astype(jnp.float32)) * inverse_root_depth
    if valid is not None:
        similarity_grid = jnp.where(valid[None, :, :], similarity_grid, jnp.float32(-1e30))
    top = jnp.max(similarity_grid, axis=-1, keepdims=True)
    weight = jnp.exp(similarity_grid - top)
    if valid is not None:
        weight = jnp.where(valid[None, :, :], weight, jnp.float32(0.0))
    total = jnp.sum(weight, axis=-1)
    focus_probabilities = weight.astype(jnp.bfloat16)
    weighted_values = jnp.einsum('xic,cxe->ixe', focus_probabilities.astype(jnp.float32), value_vectors.astype(jnp.float32))
    return (weighted_values / jnp.transpose(total)[:, :, None]).astype(jnp.bfloat16)


def reference(q_local, k_local, nearby_band_contents, q_stride, k_stride, v_stride, w_local, dilated_combiner):
    seqlen = q_local.shape[0]
    local_q = q_local.reshape(seqlen, HL, HD)
    nearby_band_keys = jnp.pad(k_local.reshape(seqlen, HL, HD), ((BAND, BAND), (0, 0), (0, 0)))
    local_v = jnp.pad(nearby_band_contents.reshape(seqlen, HL, HD), ((BAND, BAND), (0, 0), (0, 0)))

    def local_block(index):
        start = (index * TOK_DEV).astype(jnp.int32)
        requester_positions = lax.dynamic_slice_in_dim(local_q, start, TOK_DEV, 0)
        key = lax.dynamic_slice_in_dim(nearby_band_keys, start, TOK_DEV + 2 * BAND, 0)
        value_vectors = lax.dynamic_slice_in_dim(local_v, start, TOK_DEV + 2 * BAND, 0)
        qpos = start + jnp.arange(TOK_DEV, dtype=jnp.int32)
        kpos = start - BAND + jnp.arange(TOK_DEV + 2 * BAND, dtype=jnp.int32)
        valid = (jnp.abs(qpos[:, None] - kpos[None, :]) <= BAND) & (kpos[None, :] >= 0) & (kpos[None, :] < seqlen)
        return attend(requester_positions, key, value_vectors, valid)

    blocks = lax.map(local_block, jnp.arange(seqlen // TOK_DEV, dtype=jnp.int32))
    attn_local = blocks.reshape(seqlen, HL * HD)

    columns = seqlen // STRIDE

    def by_head(array):
        return jnp.moveaxis(array.reshape(columns, STRIDE, HS, HD), 2, 0)

    def single_head_view(parts):
        return attend(parts[0], parts[1], parts[2], None)

    strided = lax.map(single_head_view, (by_head(q_stride), by_head(k_stride), by_head(v_stride)))
    attn_stride = jnp.moveaxis(strided, 0, 2).reshape(seqlen, HS * HD)
    mixed = jnp.dot(attn_local, w_local, preferred_element_type=jnp.float32) + jnp.dot(attn_stride, dilated_combiner, preferred_element_type=jnp.float32)
    return mixed.astype(jnp.bfloat16)
```

```python
import functools

import jax
import jax.numpy as jnp
from jax import lax
from jax.experimental import pallas as pl
from jax.experimental.pallas import tpu as pltpu
from jax.sharding import PartitionSpec as P

HD = 128
STRIDE = 256
BAND = 256
PLANE = 4
TILE = 16
OFF = -1e30
SCALE = HD**-0.5
MIB = 1 << 20

VMEM = pl.BlockSpec(memory_space=pltpu.VMEM)
SMEM = pl.BlockSpec(memory_space=pltpu.SMEM)


def swap(array, axis, mask):
    count = lax.axis_size(axis)
    return lax.ppermute(array, axis, [(i, i ^ mask) for i in range(count)])


def scores(q, k):
    return lax.dot_general(q, k, (((1,), (1,)), ((), ())), preferred_element_type=jnp.float32)


def softmax_sum(score, v):
    top = jnp.max(score, axis=-1, keepdims=True)
    weight = jnp.exp(score - top)
    total = jnp.sum(weight, axis=-1, keepdims=True)
    out = jnp.dot(weight.astype(jnp.bfloat16), v, preferred_element_type=jnp.float32)
    return (out / total).astype(jnp.bfloat16)


def band_kernel(place_ref, q_ref, k_ref, v_ref, lows_ref, highs_ref, out_ref, k_all, v_all, bias):
    rows = q_ref.shape[0]
    step = BAND
    blocks = rows // step

    @pl.when(pl.program_id(0) == 0)
    def _():
        query = lax.broadcasted_iota(jnp.int32, (step, 3 * BAND), 0)
        key = lax.broadcasted_iota(jnp.int32, (step, 3 * BAND), 1)
        inside = (key >= query) & (key <= query + 2 * BAND)
        for b in range(blocks):
            there = inside
            if b == 0:
                there = there & ((key >= BAND) | (place_ref[0] > 0))
            if b == blocks - 1:
                there = there & ((key < 2 * BAND) | (place_ref[0] < place_ref[1] - 1))
            bias[b] = jnp.where(there, 0.0, OFF)

    for held, low, own, high in (
        (k_all, lows_ref.at[0], k_ref, highs_ref.at[0]),
        (v_all, lows_ref.at[1], v_ref, highs_ref.at[1]),
    ):
        held[:BAND] = low[...]
        held[BAND : BAND + rows] = own[...]
        held[BAND + rows :] = high[...]
    for b in range(blocks):
        at = slice(b * step, b * step + step)
        near = slice(b * step, b * step + 3 * BAND)
        score = scores(q_ref[at], k_all[near]) * SCALE + bias[b]
        out_ref[at] = softmax_sum(score, v_all[near])


def band_attention(place, q, k, v, lows, highs):
    rows, width = q.shape
    own = pl.BlockSpec((rows, HD), lambda h: (0, h))
    side = pl.BlockSpec((2, BAND, HD), lambda h: (0, 0, h))
    return pl.pallas_call(
        band_kernel,
        grid=(width // HD,),
        in_specs=[SMEM, own, own, own, side, side],
        out_specs=own,
        out_shape=jax.ShapeDtypeStruct(q.shape, q.dtype),
        scratch_shapes=[
            pltpu.VMEM((rows + 2 * BAND, HD), jnp.bfloat16),
            pltpu.VMEM((rows + 2 * BAND, HD), jnp.bfloat16),
            pltpu.VMEM((rows // BAND, BAND, 3 * BAND), jnp.float32),
        ],
        compiler_params=pltpu.CompilerParams(vmem_limit_bytes=24 * MIB),
        cost_estimate=pl.CostEstimate(
            flops=4 * rows * 3 * BAND * width,
            bytes_accessed=10 * rows * width,
            transcendentals=rows * 3 * BAND * width // HD,
        ),
        name="band_attention",
    )(place, q, k, v, lows, highs)


def column_kernel(planes, *refs):
    ins, outs = refs[:planes], refs[planes : 2 * planes]
    held, bias, result = refs[2 * planes :]
    length = held.shape[1]
    block = bias.shape[0]
    pieces = [(d, a, b, j) for d in range(planes) for a in (0, 1) for b in (0, 1) for j in (0, 1)]
    for i, (d, a, b, j) in enumerate(pieces):
        for t in range(3):
            held[t, i * TILE : (i + 1) * TILE] = ins[d][a, b, t, j]
    query = lax.broadcasted_iota(jnp.int32, bias.shape, 0)
    key = lax.broadcasted_iota(jnp.int32, bias.shape, 1)
    bias[...] = jnp.where((query & (TILE - 1)) == (key & (TILE - 1)), 0.0, OFF)

    @pl.loop(0, length // block)
    def _(step):
        at = pl.ds(pl.multiple_of(step * block, block), block)
        for h in range(held.shape[2] // HD):
            lanes = slice(h * HD, h * HD + HD)
            score = scores(held[0, at, lanes], held[1, :, lanes]) * SCALE + bias[...]
            result[at, lanes] = softmax_sum(score, held[2, :, lanes])

    for i, (d, a, b, j) in enumerate(pieces):
        outs[d][a, b, j] = result[i * TILE : (i + 1) * TILE]


def column_attention(slots):
    planes = len(slots)
    lanes = slots[0].shape[-1]
    length = planes * 8 * TILE
    block = min(length, 256)
    shape = jax.ShapeDtypeStruct((2, 2, 2, TILE, lanes), jnp.bfloat16)
    return pl.pallas_call(
        functools.partial(column_kernel, planes),
        in_specs=[VMEM] * planes,
        out_specs=[VMEM] * planes,
        out_shape=[shape] * planes,
        scratch_shapes=[
            pltpu.VMEM((3, length, lanes), jnp.bfloat16),
            pltpu.VMEM((block, length), jnp.float32),
            pltpu.VMEM((length, lanes), jnp.bfloat16),
        ],
        compiler_params=pltpu.CompilerParams(vmem_limit_bytes=40 * MIB),
        cost_estimate=pl.CostEstimate(
            flops=4 * length * length * lanes,
            bytes_accessed=8 * length * lanes,
            transcendentals=length * length * lanes // HD,
        ),
        name="column_attention",
    )(*slots)


def project_kernel(planes, place_ref, own_ref, got_ref, w_ref, local_ref, keep_ref, send_ref, rows_ref, sum_ref):
    lanes = own_ref.shape[-1]
    chunk = planes * TILE

    @pl.when(pl.program_id(0) == 0)
    def _():
        for c, held in enumerate((own_ref, got_ref)):
            for a in (0, 1):
                lane = ((place_ref[4] ^ c) * 2 + (place_ref[3] ^ a)) * lanes
                at = pl.ds(pl.multiple_of(lane, lanes), lanes)
                for d in range(planes):
                    for j in (0, 1):
                        row = j * chunk + (place_ref[2] ^ d) * TILE
                        rows_ref[pl.ds(pl.multiple_of(row, TILE), TILE), at] = held[a, d, j]

    total = jnp.dot(rows_ref[...], w_ref[...], preferred_element_type=jnp.float32)
    sum_ref[...] = total.reshape(sum_ref.shape) + local_ref[...]
    mine = place_ref[5]
    keep_ref[...] = sum_ref[mine]
    send_ref[...] = sum_ref[1 - mine].astype(jnp.bfloat16)


def project(place, own, got, w, local, index):
    planes = own.shape[1]
    chunk = planes * TILE
    depth, width = w.shape
    step = 512
    return pl.pallas_call(
        functools.partial(project_kernel, planes),
        grid=(width // step,),
        in_specs=[
            SMEM,
            pl.BlockSpec(own.shape, lambda n: (0,) * 5),
            pl.BlockSpec(own.shape, lambda n: (0,) * 5),
            pl.BlockSpec((depth, step), lambda n: (0, n)),
            pl.BlockSpec((2, chunk, step), lambda n: (0, index, n)),
        ],
        out_specs=[pl.BlockSpec((chunk, step), lambda n: (0, n))] * 2,
        out_shape=[
            jax.ShapeDtypeStruct((chunk, width), jnp.float32),
            jax.ShapeDtypeStruct((chunk, width), jnp.bfloat16),
        ],
        scratch_shapes=[
            pltpu.VMEM((2 * chunk, depth), jnp.bfloat16),
            pltpu.VMEM((2, chunk, step), jnp.float32),
        ],
        compiler_params=pltpu.CompilerParams(vmem_limit_bytes=24 * MIB),
        cost_estimate=pl.CostEstimate(
            flops=4 * chunk * depth * width,
            bytes_accessed=2 * depth * width + 14 * chunk * width,
            transcendentals=0,
        ),
        name="project",
    )(place, own, got, w, local)


def body(
    q_local, k_local, nearby_band_contents, q_stride, k_stride, v_stride, w_local, dilated_combiner
):
    rows, width = q_stride.shape
    per_column = rows // STRIDE
    count = lax.axis_size("seq")
    planes = count // PLANE
    s = lax.axis_index("seq")
    z, x, core = s // PLANE, (s // 2) % 2, s % 2
    mine = lax.axis_index("head")
    place = jnp.stack([s, jnp.int32(count), z, x, core, mine]).astype(jnp.int32)
    half, lanes = width // 2, width // PLANE
    chunk = TILE * planes
    chunks = STRIDE // chunk

    given = [lax.dynamic_slice_in_dim(a, (1 - core) * half, half, 1) for a in (q_stride, k_stride, v_stride)]
    held = [lax.dynamic_slice_in_dim(a, core * half, half, 1) for a in (q_stride, k_stride, v_stride)]
    got = swap(jnp.stack(given), "seq", 1)
    held = jnp.stack([jnp.stack(held), got]).reshape(2, 3, per_column, STRIDE, half)

    ends = jnp.stack([k_local, nearby_band_contents])
    lows = lax.ppermute(ends[:, rows - BAND :], "seq", [(i, i + 1) for i in range(count - 1)])
    highs = lax.ppermute(ends[:, :BAND], "seq", [(i + 1, i) for i in range(count - 1)])

    def over_x(i):
        part = held[:, :, :, i * chunk : (i + 1) * chunk]
        keep = lax.dynamic_slice_in_dim(part, x * lanes, lanes, 4)
        give = lax.dynamic_slice_in_dim(part, (1 - x) * lanes, lanes, 4)
        both = jnp.stack([keep, swap(give, "seq", 2)])
        return both.reshape(2, 2, 3, per_column, planes, TILE, lanes)

    def over_z(both):
        slots = []
        for d in range(planes):
            block = lax.dynamic_index_in_dim(both, z ^ d, 4, keepdims=False)
            slots.append(swap(block, "seq", d * PLANE) if d else block)
        return slots

    def back(outs):
        outs = [swap(o, "seq", d * PLANE) if d else o for d, o in enumerate(outs)]
        outs = jnp.stack(outs)
        outs = jnp.stack([outs[:, 0], swap(outs[:, 1], "seq", 2)])
        own, give = outs[:, :, 0], outs[:, :, 1]
        return own, swap(give, "seq", 1)

    attn_local = band_attention(place, q_local, k_local, nearby_band_contents, lows, highs)
    part_local = jnp.dot(attn_local, w_local, preferred_element_type=jnp.float32)
    part_local = part_local.reshape(per_column, STRIDE, -1)
    results = []
    for i in range(chunks):
        own, got = back(column_attention(over_z(over_x(i))))
        keep, send = project(place, own, got, dilated_combiner, part_local, i)
        results.append((keep + swap(send, "head", 1).astype(jnp.float32)).astype(jnp.bfloat16))
    return jnp.concatenate(results, 0)


def solution(mesh):
    in_specs = (
        P("seq", "head"),
        P("seq", "head"),
        P("seq", "head"),
        P("seq", "head"),
        P("seq", "head"),
        P("seq", "head"),
        P("head", None),
        P("head", None),
    )
    out_specs = P(("seq", "head"), None)
    return jax.shard_map(body, mesh=mesh, in_specs=in_specs, out_specs=out_specs, check_vma=False)
```

```python
import functools

import jax
import jax.numpy as jnp
from jax import lax
from jax.experimental import pallas as pl
from jax.experimental.pallas import tpu as pltpu
from jax.sharding import PartitionSpec as P

HD = 128
STRIDE = 256
BAND = 256
PLANE = 4
TILE = 16
OFF = -1e30
SCALE = HD**-0.5
LOG2E = 1.4426950408889634
MIB = 1 << 20
FREE = pl.CostEstimate(flops=0, bytes_accessed=0, transcendentals=0)

VMEM = pl.BlockSpec(memory_space=pltpu.VMEM)
SMEM = pl.BlockSpec(memory_space=pltpu.SMEM)
ANY = pl.BlockSpec(memory_space=pl.ANY)


def swap(array, axis, mask):
    count = lax.axis_size(axis)
    return lax.ppermute(array, axis, [(i, i ^ mask) for i in range(count)])


def scores(q, k):
    return lax.dot_general(q, k, (((1,), (1,)), ((), ())), preferred_element_type=jnp.float32)


def softmax_sum(score, v):
    top = jnp.max(score, axis=-1, keepdims=True)
    weight = jnp.exp2((score - top) * (SCALE * LOG2E))
    total = jnp.sum(weight, axis=-1, keepdims=True)
    out = jnp.dot(weight.astype(jnp.bfloat16), v, preferred_element_type=jnp.float32)
    return (out / total).astype(jnp.bfloat16)


def band_kernel(place_ref, q_ref, k_ref, v_ref, lows_ref, highs_ref, *refs):
    out_ref, k_all, v_all, bias = refs[-4:]
    rows = q_ref.shape[0]
    step = BAND
    blocks = rows // step

    @pl.when(pl.program_id(0) == 0)
    def _():
        query = lax.broadcasted_iota(jnp.int32, (step, BAND), 0)
        key = lax.broadcasted_iota(jnp.int32, (step, BAND), 1)
        for b in range(blocks):
            before = key >= query
            after = key <= query
            if b == 0:
                before = before & (place_ref[0] > 0)
            if b == blocks - 1:
                after = after & (place_ref[0] < place_ref[1] - 1)
            bias[b, 0] = jnp.where(before, 0.0, OFF)
            bias[b, 1] = jnp.where(after, 0.0, OFF)

    for held, low, own, high in (
        (k_all, lows_ref.at[0], k_ref, highs_ref.at[0]),
        (v_all, lows_ref.at[1], v_ref, highs_ref.at[1]),
    ):
        held[:BAND] = low[...]
        held[BAND : BAND + rows] = own[...]
        held[BAND + rows :] = high[...]
    for b in range(blocks):
        at = slice(b * step, b * step + step)
        near = slice(b * step, b * step + 3 * BAND)
        score = scores(q_ref[at], k_all[near])
        score = jnp.concatenate(
            [
                score[:, :BAND] + bias[b, 0],
                score[:, BAND : 2 * BAND],
                score[:, 2 * BAND :] + bias[b, 1],
            ],
            axis=1,
        )
        out_ref[at] = softmax_sum(score, v_all[near])


def band_attention(place, q, k, v, lows, highs, after=()):
    rows, width = q.shape
    own = pl.BlockSpec((rows, HD), lambda h: (0, h))
    side = pl.BlockSpec((2, BAND, HD), lambda h: (0, 0, h))
    return pl.pallas_call(
        band_kernel,
        grid=(width // HD,),
        in_specs=[SMEM, own, own, own, side, side] + [ANY] * len(after),
        out_specs=own,
        out_shape=jax.ShapeDtypeStruct(q.shape, q.dtype),
        scratch_shapes=[
            pltpu.VMEM((rows + 2 * BAND, HD), jnp.bfloat16),
            pltpu.VMEM((rows + 2 * BAND, HD), jnp.bfloat16),
            pltpu.VMEM((rows // BAND, 2, BAND, BAND), jnp.float32),
        ],
        compiler_params=pltpu.CompilerParams(vmem_limit_bytes=62 * MIB),
        cost_estimate=FREE,
        name="band_attention",
    )(place, q, k, v, lows, highs, *after)


def add_kernel(keep_ref, got_ref, *refs):
    refs[-1][...] = (keep_ref[...] + got_ref[...].astype(jnp.float32)).astype(jnp.bfloat16)


def add_into(out, keep, got, first, rows, after=()):
    chunk, width = keep.shape
    step = width
    spec = pl.BlockSpec((chunk, step), lambda n: (0, n))
    held = () if out is None else (out,)
    return pl.pallas_call(
        add_kernel,
        grid=(width // step,),
        in_specs=[spec, spec] + [ANY] * (len(held) + len(after)),
        out_specs=pl.BlockSpec((chunk, step), lambda n: (first // chunk, n)),
        out_shape=jax.ShapeDtypeStruct((rows, width), jnp.bfloat16),
        input_output_aliases={2: 0} if held else {},
        compiler_params=pltpu.CompilerParams(vmem_limit_bytes=62 * MIB),
        cost_estimate=FREE,
        name="add_into",
    )(keep, got, *held, *after)


def ends_kernel(k_ref, v_ref, *refs):
    lows_ref, highs_ref = refs[-2:]
    for t, held in enumerate((k_ref, v_ref)):
        highs_ref[t] = held[:BAND]
        lows_ref[t] = held[held.shape[0] - BAND :]


def ends(k, v, after=()):
    shape = jax.ShapeDtypeStruct((2, BAND, k.shape[1]), k.dtype)
    return pl.pallas_call(
        ends_kernel,
        grid=(1,),
        in_specs=[pl.BlockSpec(k.shape, lambda n: (0, 0))] * 2 + [ANY] * len(after),
        out_specs=[pl.BlockSpec(shape.shape, lambda n: (0, 0, 0))] * 2,
        out_shape=[shape] * 2,
        compiler_params=pltpu.CompilerParams(vmem_limit_bytes=62 * MIB),
        cost_estimate=FREE,
        name="ends",
    )(k, v, *after)


def pack_kernel(q_ref, k_ref, v_ref, *refs):
    out_ref = refs[-1]
    per_column, tile, _ = q_ref.shape
    lanes = out_ref.shape[-1]
    ahead = out_ref.shape[1] - 3 * per_column * tile
    for p in range(PLANE):
        for t, held in enumerate((q_ref, k_ref, v_ref)):
            for j in range(per_column):
                at = ahead + (t * per_column + j) * tile
                out_ref[p, at : at + tile] = held[j, :, p * lanes : (p + 1) * lanes]


def pack(arrays, first, tile, ahead, planes, after=()):
    rows, width = arrays[0].shape
    per_column = rows // STRIDE
    lanes = width // PLANE
    views = [a.reshape(per_column, STRIDE, width) for a in arrays]
    spec = pl.BlockSpec((per_column, tile, width), lambda n: (0, first // tile + n, 0))
    shape = (planes * PLANE, ahead + 3 * per_column * tile, lanes)
    return pl.pallas_call(
        pack_kernel,
        grid=(planes,),
        in_specs=[spec] * 3 + [ANY] * len(after),
        out_specs=pl.BlockSpec((PLANE,) + shape[1:], lambda n: (n, 0, 0)),
        out_shape=jax.ShapeDtypeStruct(shape, jnp.bfloat16),
        compiler_params=pltpu.CompilerParams(vmem_limit_bytes=62 * MIB),
        cost_estimate=FREE,
        name="pack",
    )(*views, *after)


def column_kernel(tile, ahead, in_ref, *refs):
    out_ref, held, bias, result = refs[-4:]
    count = in_ref.shape[0]
    per_column = out_ref.shape[1] // tile
    length = held.shape[1]
    block = bias.shape[0]

    @pl.when(pl.program_id(0) == 0)
    def _():
        query = lax.broadcasted_iota(jnp.int32, bias.shape, 0)
        key = lax.broadcasted_iota(jnp.int32, bias.shape, 1)
        bias[...] = jnp.where((query & (TILE - 1)) == (key & (TILE - 1)), 0.0, OFF)

    for part in range(tile // TILE):
        for s in range(count):
            for j in range(per_column):
                at = (s * per_column + j) * TILE
                for t in range(3):
                    row = ahead + (t * per_column + j) * tile + part * TILE
                    held[t, at : at + TILE] = in_ref[s, row : row + TILE]

        @pl.loop(0, length // block)
        def _(step):
            at = pl.ds(pl.multiple_of(step * block, block), block)
            score = scores(held[0, at], held[1]) + bias[...]
            result[at] = softmax_sum(score, held[2])

        for s in range(count):
            for j in range(per_column):
                at = (s * per_column + j) * TILE
                row = j * tile + part * TILE
                out_ref[s, row : row + TILE] = result[at : at + TILE]


def column_attention(got, ahead, tile, per_column, into, after=()):
    count, rows, lanes = got.shape
    length = count * per_column * TILE
    block = min(length, 256)
    held = () if into is None else (into,)
    shape = (count, per_column * tile, lanes) if into is None else into.shape
    return pl.pallas_call(
        functools.partial(column_kernel, tile, ahead),
        grid=(lanes // HD,),
        in_specs=[pl.BlockSpec((count, rows, HD), lambda h: (0, 0, h))]
        + [ANY] * (len(held) + len(after)),
        out_specs=pl.BlockSpec((count, per_column * tile, HD), lambda h: (0, 0, h)),
        out_shape=jax.ShapeDtypeStruct(shape, jnp.bfloat16),
        input_output_aliases={1: 0} if held else {},
        scratch_shapes=[
            pltpu.VMEM((3, length, HD), jnp.bfloat16),
            pltpu.VMEM((block, length), jnp.float32),
            pltpu.VMEM((length, HD), jnp.bfloat16),
        ],
        compiler_params=pltpu.CompilerParams(vmem_limit_bytes=62 * MIB),
        cost_estimate=FREE,
        name="column_attention",
    )(got, *held, *after)


def stream(step, w_ref, held, sems):
    width = held.shape[2]

    def block(n):
        columns = pl.ds(n * width, width)
        return pltpu.make_async_copy(w_ref.at[:, columns], held.at[n], sems.at[n])

    @pl.when(step == 0)
    def _():
        for n in range(held.shape[0]):
            block(n).start()

    for n in range(held.shape[0]):

        @pl.when(step == n)
        def _():
            block(n).wait()


def stream_scratch(depth, width, step):
    return [
        pltpu.VMEM((width // step, depth, step), jnp.bfloat16),
        pltpu.SemaphoreType.DMA((width // step,)),
    ]


def project_kernel(tile, mine_ref, w_ref, local_ref, in_ref, *refs):
    keep_ref, send_ref, rows_ref, sum_ref, held, sems = refs[-6:]
    stream(pl.program_id(0), w_ref, held, sems)

    @pl.when(pl.program_id(0) == 0)
    def _():
        count, rows, lanes = in_ref.shape
        chunk = tile * (count // PLANE)
        for s in range(count):
            lane = s % PLANE * lanes
            for j in range(rows // tile):
                row = j * chunk + s // PLANE * tile
                part = in_ref[s, j * tile : (j + 1) * tile]
                rows_ref[row : row + tile, lane : lane + lanes] = part

    w = held[pl.program_id(0)]
    total = jnp.dot(rows_ref[...], w, preferred_element_type=jnp.float32)
    sum_ref[...] = total.reshape(sum_ref.shape) + local_ref[...]
    mine = mine_ref[0]
    keep_ref[...] = sum_ref[mine]
    send_ref[...] = sum_ref[1 - mine].astype(jnp.bfloat16)


def project(mine, got, w, local, first, tile, chunk, after=()):
    depth, width = w.shape
    count, _, lanes = got.shape
    per_column = local.shape[0]
    step = 1024
    return pl.pallas_call(
        functools.partial(project_kernel, tile),
        grid=(width // step,),
        in_specs=[
            SMEM,
            ANY,
            pl.BlockSpec((per_column, chunk, step), lambda n: (0, first // chunk, n)),
            pl.BlockSpec((count, per_column * tile, lanes), lambda n: (0, 0, 0)),
        ]
        + [ANY] * len(after),
        out_specs=[pl.BlockSpec((chunk, step), lambda n: (0, n))] * 2,
        out_shape=[
            jax.ShapeDtypeStruct((chunk, width), jnp.float32),
            jax.ShapeDtypeStruct((chunk, width), jnp.bfloat16),
        ],
        scratch_shapes=[
            pltpu.VMEM((2 * chunk, depth), jnp.bfloat16),
            pltpu.VMEM((2, chunk, step), jnp.float32),
            *stream_scratch(depth, width, step),
        ],
        compiler_params=pltpu.CompilerParams(vmem_limit_bytes=62 * MIB),
        cost_estimate=FREE,
        name="project",
    )(mine, w, local, got, *after)


def local_kernel(a_ref, w_ref, *refs):
    out_ref, held, sems = refs[-3:]
    stream(pl.program_id(0), w_ref, held, sems)
    w = held[pl.program_id(0)]
    out_ref[...] = jnp.dot(a_ref[...], w, preferred_element_type=jnp.float32)


def project_local(a, w, after=()):
    rows, depth = a.shape
    width = w.shape[1]
    step = 1024
    return pl.pallas_call(
        local_kernel,
        grid=(width // step,),
        in_specs=[
            pl.BlockSpec((rows, depth), lambda n: (0, 0)),
            ANY,
        ]
        + [ANY] * len(after),
        out_specs=pl.BlockSpec((rows, step), lambda n: (0, n)),
        out_shape=jax.ShapeDtypeStruct((rows, width), jnp.float32),
        scratch_shapes=stream_scratch(depth, width, step),
        compiler_params=pltpu.CompilerParams(vmem_limit_bytes=62 * MIB),
        cost_estimate=FREE,
        name="project_local",
    )(a, w, *after)


def column_chunks(planes):
    tiles = STRIDE // (planes * TILE)
    if tiles == 4:
        return ((0, 2 * TILE), (2 * TILE * planes, TILE), (3 * TILE * planes, TILE))
    return tuple((i * TILE * planes, TILE) for i in range(tiles))


def body(
    q_local, k_local, nearby_band_contents, q_stride, k_stride, v_stride, w_local, dilated_combiner
):
    rows, width = q_stride.shape
    per_column = rows // STRIDE
    count = lax.axis_size("seq")
    planes = count // PLANE
    place = jnp.stack([lax.axis_index("seq"), jnp.int32(count)]).astype(jnp.int32)
    mine = lax.axis_index("head").astype(jnp.int32).reshape(1)
    chunks = column_chunks(planes)
    last = len(chunks) - 1

    def exchange(a):
        return lax.all_to_all(a, "seq", split_axis=0, concat_axis=0, tiled=True)

    stride = (q_stride, k_stride, v_stride)
    ahead = [0] + [per_column * t for _, t in chunks[:-1]]
    packed, token = [], ()
    for i, (first, tile) in enumerate(chunks):
        packed.append(pack(stride, first, tile, ahead[i], planes, token))
        if i == 0:
            lows, highs = ends(k_local, nearby_band_contents, tuple(packed))
            token = (lows,)
    packed.append(None)
    lows = lax.ppermute(lows, "seq", [(i, i + 1) for i in range(count - 1)])
    highs = lax.ppermute(highs, "seq", [(i + 1, i) for i in range(count - 1)])

    results, after = [], (lows, highs)
    got = exchange(packed[0])
    for i, (first, tile) in enumerate(chunks):
        if i == min(1, last):
            attn_local = band_attention(
                place, q_local, k_local, nearby_band_contents, lows, highs, after
            )
            part_local = project_local(attn_local, w_local, (attn_local,))
            part_local = part_local.reshape(per_column, STRIDE, -1)
            after = (part_local,)
        outs = column_attention(got, ahead[i], tile, per_column, packed[i + 1], after)
        after = (outs,)
        back, got = got, exchange(outs)
        for j in range(i - 1, i + (i == last)):
            if j < 0:
                continue
            start, tile = chunks[j]
            keep, send = project(
                mine,
                back if j < i else got,
                dilated_combiner,
                part_local,
                start,
                tile,
                tile * planes,
                after,
            )
            after = (send,)
            results.append((keep, swap(send, "head", 1), start))
    out = None
    for keep, other, start in results:
        out = add_into(out, keep, other, start, rows // 2, after if out is None else ())
    return out


def solution(mesh):
    in_specs = (
        P("seq", "head"),
        P("seq", "head"),
        P("seq", "head"),
        P("seq", "head"),
        P("seq", "head"),
        P("seq", "head"),
        P("head", None),
        P("head", None),
    )
    out_specs = P(("seq", "head"), None)
    return jax.shard_map(body, mesh=mesh, in_specs=in_specs, out_specs=out_specs, check_vma=False)
```

```python
import functools

import jax
import jax.numpy as jnp
from jax import lax
from jax.experimental import pallas as pl
from jax.experimental.pallas import tpu as pltpu
from jax.sharding import PartitionSpec as P

HD = 128
STRIDE = 256
BAND = 256
PLANE = 4
TILE = 8
PIECE = 16
ROUNDS = ((0, 4), (128, 2), (192, 2))
OFF = -1e30
SCALE = HD**-0.5
LOG2E = 1.4426950408889634
MIB = 1 << 20
FREE = pl.CostEstimate(flops=0, bytes_accessed=0, transcendentals=0)

VMEM = pl.BlockSpec(memory_space=pltpu.VMEM)
SMEM = pl.BlockSpec(memory_space=pltpu.SMEM)
ANY = pl.BlockSpec(memory_space=pl.ANY)


def swap(array, axis, mask):
    count = lax.axis_size(axis)
    return lax.ppermute(array, axis, [(i, i ^ mask) for i in range(count)])


def scores(q, k):
    return lax.dot_general(q, k, (((1,), (1,)), ((), ())), preferred_element_type=jnp.float32)


def softmax_sum(score, v):
    top = jnp.max(score, axis=-1, keepdims=True)
    weight = jnp.exp2((score - top) * (SCALE * LOG2E))
    total = jnp.sum(weight, axis=-1, keepdims=True)
    out = jnp.dot(weight.astype(jnp.bfloat16), v, preferred_element_type=jnp.float32)
    return (out / total).astype(jnp.bfloat16)


def band_kernel(place_ref, q_ref, k_ref, v_ref, lows_ref, highs_ref, *refs):
    out_ref, k_all, v_all, bias = refs[-4:]
    rows = q_ref.shape[0]
    step = BAND
    blocks = rows // step

    @pl.when(pl.program_id(0) == 0)
    def _():
        query = lax.broadcasted_iota(jnp.int32, (step, BAND), 0)
        key = lax.broadcasted_iota(jnp.int32, (step, BAND), 1)
        for b in range(blocks):
            before = key >= query
            after = key <= query
            if b == 0:
                before = before & (place_ref[0] > 0)
            if b == blocks - 1:
                after = after & (place_ref[0] < place_ref[1] - 1)
            bias[b, 0] = jnp.where(before, 0.0, OFF)
            bias[b, 1] = jnp.where(after, 0.0, OFF)

    for held, low, own, high in (
        (k_all, lows_ref.at[0], k_ref, highs_ref.at[0]),
        (v_all, lows_ref.at[1], v_ref, highs_ref.at[1]),
    ):
        held[:BAND] = low[...]
        held[BAND : BAND + rows] = own[...]
        held[BAND + rows :] = high[...]
    for b in range(blocks):
        at = slice(b * step, b * step + step)
        near = slice(b * step, b * step + 3 * BAND)
        score = scores(q_ref[at], k_all[near])
        score = jnp.concatenate(
            [
                score[:, :BAND] + bias[b, 0],
                score[:, BAND : 2 * BAND],
                score[:, 2 * BAND :] + bias[b, 1],
            ],
            axis=1,
        )
        out_ref[at] = softmax_sum(score, v_all[near])


def band_attention(place, q, k, v, lows, highs, after=()):
    rows, width = q.shape
    own = pl.BlockSpec((rows, HD), lambda h: (0, h))
    side = pl.BlockSpec((2, BAND, HD), lambda h: (0, 0, h))
    return pl.pallas_call(
        band_kernel,
        grid=(width // HD,),
        in_specs=[SMEM, own, own, own, side, side] + [ANY] * len(after),
        out_specs=own,
        out_shape=jax.ShapeDtypeStruct(q.shape, q.dtype),
        scratch_shapes=[
            pltpu.VMEM((rows + 2 * BAND, HD), jnp.bfloat16),
            pltpu.VMEM((rows + 2 * BAND, HD), jnp.bfloat16),
            pltpu.VMEM((rows // BAND, 2, BAND, BAND), jnp.float32),
        ],
        compiler_params=pltpu.CompilerParams(vmem_limit_bytes=60 * MIB),
        cost_estimate=FREE,
        name="band_attention",
    )(place, q, k, v, lows, highs, *after)


def add_kernel(keep_ref, got_ref, *refs):
    refs[-1][...] = (keep_ref[...] + got_ref[...].astype(jnp.float32)).astype(jnp.bfloat16)


def add_into(out, keep, got, first, part, parts, rows, after=()):
    chunk, width = keep.shape
    step = width
    spec = pl.BlockSpec((chunk, step), lambda n: (0, n))
    held = () if out is None else (out,)
    return pl.pallas_call(
        add_kernel,
        grid=(width // step,),
        in_specs=[spec, spec] + [ANY] * (len(held) + len(after)),
        out_specs=pl.BlockSpec((chunk, step), lambda n: (first // chunk, part)),
        out_shape=jax.ShapeDtypeStruct((rows, parts * width), jnp.bfloat16),
        input_output_aliases={2: 0} if held else {},
        compiler_params=pltpu.CompilerParams(vmem_limit_bytes=16 * MIB),
        cost_estimate=FREE,
        name="add_into",
    )(keep, got, *held, *after)


def ends_kernel(k_ref, v_ref, *refs):
    lows_ref, highs_ref = refs[-2:]
    for t, held in enumerate((k_ref, v_ref)):
        highs_ref[t] = held[:BAND]
        lows_ref[t] = held[held.shape[0] - BAND :]


def ends(k, v, after=()):
    shape = jax.ShapeDtypeStruct((2, BAND, k.shape[1]), k.dtype)
    return pl.pallas_call(
        ends_kernel,
        grid=(1,),
        in_specs=[pl.BlockSpec(k.shape, lambda n: (0, 0))] * 2 + [ANY] * len(after),
        out_specs=[pl.BlockSpec(shape.shape, lambda n: (0, 0, 0))] * 2,
        out_shape=[shape] * 2,
        compiler_params=pltpu.CompilerParams(vmem_limit_bytes=60 * MIB),
        cost_estimate=FREE,
        name="ends",
    )(k, v, *after)


def pack_kernel(planes, ahead, q_ref, k_ref, v_ref, *refs):
    out_ref = refs[-1]
    lanes = out_ref.shape[-1]
    per_column, columns, _ = q_ref.shape
    unit = pl.program_id(0)
    for t, held in enumerate((q_ref, k_ref, v_ref)):
        rows = [held[j].astype(jnp.float32) for j in range(per_column)]
        at = pl.ds(pl.multiple_of(ahead + (unit * 3 + t) * PIECE, PIECE), PIECE)
        for z in range(planes):
            piece = jnp.concatenate([r[z * TILE : (z + 1) * TILE] for r in rows])
            piece = piece.astype(jnp.bfloat16)
            for p in range(PLANE):
                out_ref[z * PLANE + p, at] = piece[:, p * lanes : (p + 1) * lanes]


def pack(arrays, first, units, ahead, planes, after=()):
    rows, width = arrays[0].shape
    per_column = rows // STRIDE
    lanes = width // PLANE
    columns = planes * TILE
    views = [a.reshape(per_column, STRIDE, width) for a in arrays]
    spec = pl.BlockSpec((per_column, columns, width), lambda n: (0, first // columns + n, 0))
    shape = (planes * PLANE, ahead + 3 * PIECE * units, lanes)
    return pl.pallas_call(
        functools.partial(pack_kernel, planes, ahead),
        grid=(units,),
        in_specs=[spec] * 3 + [ANY] * len(after),
        out_specs=pl.BlockSpec(shape, lambda n: (0, 0, 0)),
        out_shape=jax.ShapeDtypeStruct(shape, jnp.bfloat16),
        compiler_params=pltpu.CompilerParams(vmem_limit_bytes=60 * MIB),
        cost_estimate=FREE,
        name="pack",
    )(*views, *after)


def column_kernel(lo, units, ahead, in_ref, *refs):
    out_ref, held, result, bias, in_sems, out_sems = refs[-6:]
    count, lanes = held.shape[2], held.shape[4]
    length = count * PIECE
    block = bias.shape[0]

    def arrival(u, t):
        rows = pl.ds(ahead + ((lo + u) * 3 + t) * PIECE, PIECE)
        return pltpu.make_async_copy(in_ref.at[:, rows], held.at[u, t], in_sems.at[u, t])

    def departure(u):
        rows = pl.ds((lo + u) * PIECE, PIECE)
        return pltpu.make_async_copy(result.at[u], out_ref.at[:, rows], out_sems.at[u])

    for u in range(units):
        for t in range(3):
            arrival(u, t).start()
    query = lax.broadcasted_iota(jnp.int32, bias.shape, 0)
    key = lax.broadcasted_iota(jnp.int32, bias.shape, 1)
    bias[...] = jnp.where((query & (TILE - 1)) == (key & (TILE - 1)), 0.0, OFF)
    for u in range(units):
        for t in range(3):
            arrival(u, t).wait()
        for h in range(lanes // HD):
            head = slice(h * HD, h * HD + HD)
            k = held[u, 1, :, :, head].reshape(length, HD)
            v = held[u, 2, :, :, head].reshape(length, HD)
            for s in range(0, count, block // PIECE):
                part = slice(s, s + block // PIECE)
                q = held[u, 0, part, :, head].reshape(block, HD)
                out = softmax_sum(scores(q, k) + bias[...], v)
                result[u, part, :, head] = out.reshape(block // PIECE, PIECE, HD)
        departure(u).start()
    for u in range(units):
        departure(u).wait()


def column_attention(got, ahead, lo, units, into, after=()):
    count, _, lanes = got.shape
    length = count * PIECE
    block = min(length, 256)
    held = () if into is None else (into,)
    shape = (count, units * PIECE, lanes) if into is None else into.shape
    return pl.pallas_call(
        functools.partial(column_kernel, lo, units, ahead),
        in_specs=[ANY] * (1 + len(held) + len(after)),
        out_specs=ANY,
        out_shape=jax.ShapeDtypeStruct(shape, jnp.bfloat16),
        input_output_aliases={1: 0} if held else {},
        scratch_shapes=[
            pltpu.VMEM((units, 3, count, PIECE, lanes), jnp.bfloat16),
            pltpu.VMEM((units, count, PIECE, lanes), jnp.bfloat16),
            pltpu.VMEM((block, length), jnp.float32),
            pltpu.SemaphoreType.DMA((units, 3)),
            pltpu.SemaphoreType.DMA((units,)),
        ],
        compiler_params=pltpu.CompilerParams(vmem_limit_bytes=52 * MIB),
        cost_estimate=FREE,
        name="column_attention",
    )(got, *held, *after)


def stream(step, w_ref, held, sems, start=0):
    width = held.shape[2]

    def block(n):
        columns = pl.ds(start + n * width, width)
        return pltpu.make_async_copy(w_ref.at[:, columns], held.at[n], sems.at[n])

    @pl.when(step == 0)
    def _():
        for n in range(held.shape[0]):
            block(n).start()

    for n in range(held.shape[0]):

        @pl.when(step == n)
        def _():
            block(n).wait()


def stream_scratch(depth, width, step):
    return [
        pltpu.VMEM((width // step, depth, step), jnp.bfloat16),
        pltpu.SemaphoreType.DMA((width // step,)),
    ]


def project_kernel(units, begin, mine_ref, w_ref, local_ref, in_ref, *refs):
    keep_ref, send_ref, rows_ref, sum_ref, held, sems = refs[-6:]
    stream(pl.program_id(0), w_ref, held, sems, begin)

    @pl.when(pl.program_id(0) == 0)
    def _():
        count, _, lanes = in_ref.shape
        planes = count // PLANE
        columns = planes * TILE
        chunk = units * columns
        for u in range(units):
            for p in range(PLANE):
                pieces = [
                    in_ref[z * PLANE + p, u * PIECE : (u + 1) * PIECE].astype(jnp.float32)
                    for z in range(planes)
                ]
                for j in range(PIECE // TILE):
                    part = jnp.concatenate([x[j * TILE : (j + 1) * TILE] for x in pieces])
                    row = j * chunk + u * columns
                    lane = slice(p * lanes, (p + 1) * lanes)
                    rows_ref[row : row + columns, lane] = part.astype(jnp.bfloat16)

    w = held[pl.program_id(0)]
    total = jnp.dot(rows_ref[...], w, preferred_element_type=jnp.float32)
    sum_ref[...] = total.reshape(sum_ref.shape) + local_ref[...]
    mine = mine_ref[0]
    keep_ref[...] = sum_ref[mine]
    send_ref[...] = sum_ref[1 - mine].astype(jnp.bfloat16)


def project(mine, got, w, local, first, units, chunk, part, parts, after=()):
    depth = w.shape[0]
    width = w.shape[1] // parts
    count, _, lanes = got.shape
    per_column = local.shape[0]
    step = 1024
    steps = width // step
    return pl.pallas_call(
        functools.partial(project_kernel, units, part * width),
        grid=(width // step,),
        in_specs=[
            SMEM,
            ANY,
            pl.BlockSpec((per_column, chunk, step), lambda n: (0, first // chunk, part * steps + n)),
            pl.BlockSpec((count, units * PIECE, lanes), lambda n: (0, 0, 0)),
        ]
        + [ANY] * len(after),
        out_specs=[pl.BlockSpec((chunk, step), lambda n: (0, n))] * 2,
        out_shape=[
            jax.ShapeDtypeStruct((chunk, width), jnp.float32),
            jax.ShapeDtypeStruct((chunk, width), jnp.bfloat16),
        ],
        scratch_shapes=[
            pltpu.VMEM((2 * chunk, depth), jnp.bfloat16),
            pltpu.VMEM((2, chunk, step), jnp.float32),
            *stream_scratch(depth, width, step),
        ],
        compiler_params=pltpu.CompilerParams(vmem_limit_bytes=58 * MIB),
        cost_estimate=FREE,
        name="project",
    )(mine, w, local, got, *after)


def local_kernel(a_ref, w_ref, *refs):
    out_ref, held, sems = refs[-3:]
    stream(pl.program_id(0), w_ref, held, sems)
    w = held[pl.program_id(0)]
    out_ref[...] = jnp.dot(a_ref[...], w, preferred_element_type=jnp.float32)


def project_local(a, w, after=()):
    rows, depth = a.shape
    width = w.shape[1]
    step = 1024
    return pl.pallas_call(
        local_kernel,
        grid=(width // step,),
        in_specs=[
            pl.BlockSpec((rows, depth), lambda n: (0, 0)),
            ANY,
        ]
        + [ANY] * len(after),
        out_specs=pl.BlockSpec((rows, step), lambda n: (0, n)),
        out_shape=jax.ShapeDtypeStruct((rows, width), jnp.float32),
        scratch_shapes=stream_scratch(depth, width, step),
        compiler_params=pltpu.CompilerParams(vmem_limit_bytes=60 * MIB),
        cost_estimate=FREE,
        name="project_local",
    )(a, w, *after)


def column_chunks(planes):
    units = STRIDE // (planes * TILE)
    if units == 8:
        return ROUNDS
    return ((0, units),)


def body(
    q_local, k_local, nearby_band_contents, q_stride, k_stride, v_stride, w_local, dilated_combiner
):
    rows, width = q_stride.shape
    per_column = rows // STRIDE
    count = lax.axis_size("seq")
    planes = count // PLANE
    place = jnp.stack([lax.axis_index("seq"), jnp.int32(count)]).astype(jnp.int32)
    mine = lax.axis_index("head").astype(jnp.int32).reshape(1)
    chunks = column_chunks(planes)
    last = len(chunks) - 1

    def exchange(a):
        return lax.all_to_all(a, "seq", split_axis=0, concat_axis=0, tiled=True)

    stride = (q_stride, k_stride, v_stride)
    ahead = [0] + [PIECE * units for _, units in chunks[:-1]]
    packed, token = [], ()
    for i, (first, units) in enumerate(chunks):
        packed.append(pack(stride, first, units, ahead[i], planes, token))
        if i == 0:
            lows, highs = ends(k_local, nearby_band_contents, tuple(packed))
            token = (lows,)
    packed.append(None)
    lows = lax.ppermute(lows, "seq", [(i, i + 1) for i in range(count - 1)])
    highs = lax.ppermute(highs, "seq", [(i + 1, i) for i in range(count - 1)])

    results, after = [], (lows, highs)
    got = exchange(packed[0])
    for i, (first, units) in enumerate(chunks):
        if i == min(1, last):
            attn_local = band_attention(
                place, q_local, k_local, nearby_band_contents, lows, highs, after
            )
            part_local = project_local(attn_local, w_local, (attn_local,))
            part_local = part_local.reshape(per_column, STRIDE, -1)
            after = (part_local,)
        if i == 0 and i < last:
            early = units // 2
            outs = column_attention(got, ahead[i], 0, early, packed[i + 1])
            outs = column_attention(got, ahead[i], early, units - early, outs, after)
        else:
            outs = column_attention(got, ahead[i], 0, units, packed[i + 1], after)
        after = (outs,)
        back, got = got, exchange(outs)
        for j in range(i - 1, i + (i == last)):
            if j < 0:
                continue
            start, size = chunks[j]
            parts = 2 if j == last else 1
            for part in range(parts):
                keep, send = project(
                    mine,
                    back if j < i else got,
                    dilated_combiner,
                    part_local,
                    start,
                    size,
                    size * planes * TILE,
                    part,
                    parts,
                    after,
                )
                after = (send,)
                results.append((keep, swap(send, "head", 1), start, part, parts))
    out = None
    for keep, other, start, part, parts in results:
        out = add_into(out, keep, other, start, part, parts, rows // 2, after if out is None else ())
    return out


def solution(mesh):
    in_specs = (
        P("seq", "head"),
        P("seq", "head"),
        P("seq", "head"),
        P("seq", "head"),
        P("seq", "head"),
        P("seq", "head"),
        P("head", None),
        P("head", None),
    )
    out_specs = P(("seq", "head"), None)
    return jax.shard_map(body, mesh=mesh, in_specs=in_specs, out_specs=out_specs, check_vma=False)
```

```python
import functools

import jax
import jax.numpy as jnp
from jax import lax
from jax.experimental import pallas as pl
from jax.experimental.pallas import tpu as pltpu
from jax.sharding import PartitionSpec as P

HD = 128
STRIDE = 256
BAND = 256
PLANE = 4
TILE = 8
PIECE = 16
ROUNDS = ((0, 4), (128, 2), (192, 2))
OFF = -1e30
SCALE = HD**-0.5
LOG2E = 1.4426950408889634
MIB = 1 << 20
FREE = pl.CostEstimate(flops=0, bytes_accessed=0, transcendentals=0)

VMEM = pl.BlockSpec(memory_space=pltpu.VMEM)
SMEM = pl.BlockSpec(memory_space=pltpu.SMEM)
ANY = pl.BlockSpec(memory_space=pl.ANY)


def swap(array, axis, mask):
    count = lax.axis_size(axis)
    return lax.ppermute(array, axis, [(i, i ^ mask) for i in range(count)])


def scores(q, k):
    return lax.dot_general(q, k, (((1,), (1,)), ((), ())), preferred_element_type=jnp.float32)


def softmax_sum(score, v):
    top = jnp.max(score, axis=-1, keepdims=True)
    weight = jnp.exp2((score - top) * (SCALE * LOG2E))
    total = jnp.sum(weight, axis=-1, keepdims=True)
    out = jnp.dot(weight.astype(jnp.bfloat16), v, preferred_element_type=jnp.float32)
    return (out / total).astype(jnp.bfloat16)


def band_kernel(place_ref, q_ref, k_ref, v_ref, k_low, k_high, v_low, v_high, *refs):
    out_ref, k_all, v_all, bias = refs[-4:]
    rows = q_ref.shape[0]
    step = BAND
    blocks = rows // step

    @pl.when(pl.program_id(0) == 0)
    def _():
        query = lax.broadcasted_iota(jnp.int32, (step, BAND), 0)
        key = lax.broadcasted_iota(jnp.int32, (step, BAND), 1)
        for b in range(blocks):
            before = key >= query
            after = key <= query
            if b == 0:
                before = before & (place_ref[0] > 0)
            if b == blocks - 1:
                after = after & (place_ref[0] < place_ref[1] - 1)
            bias[b, 0] = jnp.where(before, 0.0, OFF)
            bias[b, 1] = jnp.where(after, 0.0, OFF)

    for held, low, own, high in (
        (k_all, k_low, k_ref, k_high),
        (v_all, v_low, v_ref, v_high),
    ):
        held[:BAND] = low[...]
        held[BAND : BAND + rows] = own[...]
        held[BAND + rows :] = high[...]
    for b in range(blocks):
        at = slice(b * step, b * step + step)
        near = slice(b * step, b * step + 3 * BAND)
        score = scores(q_ref[at], k_all[near])
        score = jnp.concatenate(
            [
                score[:, :BAND] + bias[b, 0],
                score[:, BAND : 2 * BAND],
                score[:, 2 * BAND :] + bias[b, 1],
            ],
            axis=1,
        )
        out_ref[at] = softmax_sum(score, v_all[near])


def band_attention(place, q, k, v, halos, after=()):
    rows, width = q.shape
    own = pl.BlockSpec((rows, HD), lambda h: (0, h))
    side = pl.BlockSpec((BAND, HD), lambda h: (0, h))
    return pl.pallas_call(
        band_kernel,
        grid=(width // HD,),
        in_specs=[SMEM, own, own, own, side, side, side, side] + [ANY] * len(after),
        out_specs=own,
        out_shape=jax.ShapeDtypeStruct(q.shape, q.dtype),
        scratch_shapes=[
            pltpu.VMEM((rows + 2 * BAND, HD), jnp.bfloat16),
            pltpu.VMEM((rows + 2 * BAND, HD), jnp.bfloat16),
            pltpu.VMEM((rows // BAND, 2, BAND, BAND), jnp.float32),
        ],
        compiler_params=pltpu.CompilerParams(vmem_limit_bytes=60 * MIB),
        cost_estimate=FREE,
        name="band_attention",
    )(place, q, k, v, *halos, *after)


def tie_kernel(*refs):
    pass


def tie(array, *after):
    return pl.pallas_call(
        tie_kernel,
        in_specs=[ANY] * (1 + len(after)),
        out_specs=ANY,
        out_shape=jax.ShapeDtypeStruct(array.shape, array.dtype),
        input_output_aliases={0: 0},
        compiler_params=pltpu.CompilerParams(vmem_limit_bytes=52 * MIB),
        cost_estimate=FREE,
        name="tie",
    )(array, *after)


def add_kernel(keep_ref, got_ref, *refs):
    refs[-1][...] = (keep_ref[...] + got_ref[...].astype(jnp.float32)).astype(jnp.bfloat16)


def add_into(out, keep, got, first, part, parts, rows, after=()):
    chunk, width = keep.shape
    step = width
    spec = pl.BlockSpec((chunk, step), lambda n: (0, n))
    held = () if out is None else (out,)
    return pl.pallas_call(
        add_kernel,
        grid=(width // step,),
        in_specs=[spec, spec] + [ANY] * (len(held) + len(after)),
        out_specs=pl.BlockSpec((chunk, step), lambda n: (first // chunk, part)),
        out_shape=jax.ShapeDtypeStruct((rows, parts * width), jnp.bfloat16),
        input_output_aliases={2: 0} if held else {},
        compiler_params=pltpu.CompilerParams(vmem_limit_bytes=16 * MIB),
        cost_estimate=FREE,
        name="add_into",
    )(keep, got, *held, *after)


def ends_kernel(k_ref, v_ref, *refs):
    k_low, k_high, v_low, v_high = refs[-4:]
    for held, low, high in ((k_ref, k_low, k_high), (v_ref, v_low, v_high)):
        low[...] = held[held.shape[0] - BAND :]
        high[...] = held[:BAND]


def ends(k, v, after=()):
    shape = jax.ShapeDtypeStruct((BAND, k.shape[1]), k.dtype)
    return pl.pallas_call(
        ends_kernel,
        grid=(1,),
        in_specs=[pl.BlockSpec(k.shape, lambda n: (0, 0))] * 2 + [ANY] * len(after),
        out_specs=[pl.BlockSpec(shape.shape, lambda n: (0, 0))] * 4,
        out_shape=[shape] * 4,
        compiler_params=pltpu.CompilerParams(vmem_limit_bytes=60 * MIB),
        cost_estimate=FREE,
        name="ends",
    )(k, v, *after)


def direct(low, high):
    count = lax.axis_size("seq")
    return (
        lax.ppermute(low, "seq", [(i, i + 1) for i in range(count - 1)]),
        lax.ppermute(high, "seq", [(i + 1, i) for i in range(count - 1)]),
    )


def pack_kernel(planes, ahead, q_ref, k_ref, v_ref, *refs):
    out_ref = refs[-1]
    lanes = out_ref.shape[-1]
    per_column, columns, _ = q_ref.shape
    many = columns // (planes * TILE)
    for i, t in [(i, t) for i in range(many) for t in range(3)]:
        held = (q_ref, k_ref, v_ref)[t]
        unit = pl.program_id(0) * many + i
        group = slice(i * planes * TILE, (i + 1) * planes * TILE)
        rows = [held[j, group].astype(jnp.float32) for j in range(per_column)]
        at = pl.ds(pl.multiple_of(ahead + (unit * 3 + t) * PIECE, PIECE), PIECE)
        for z in range(planes):
            piece = jnp.concatenate([r[z * TILE : (z + 1) * TILE] for r in rows])
            piece = piece.astype(jnp.bfloat16)
            for p in range(PLANE):
                out_ref[z * PLANE + p, at] = piece[:, p * lanes : (p + 1) * lanes]


def pack(arrays, first, units, ahead, planes, after=()):
    rows, width = arrays[0].shape
    per_column = rows // STRIDE
    lanes = width // PLANE
    columns = 2 * planes * TILE
    views = [a.reshape(per_column, STRIDE, width) for a in arrays]
    spec = pl.BlockSpec((per_column, columns, width), lambda n: (0, first // columns + n, 0))
    shape = (planes * PLANE, ahead + 3 * PIECE * units, lanes)
    return pl.pallas_call(
        functools.partial(pack_kernel, planes, ahead),
        grid=(units // 2,),
        in_specs=[spec] * 3 + [ANY] * len(after),
        out_specs=pl.BlockSpec(shape, lambda n: (0, 0, 0)),
        out_shape=jax.ShapeDtypeStruct(shape, jnp.bfloat16),
        compiler_params=pltpu.CompilerParams(vmem_limit_bytes=60 * MIB),
        cost_estimate=FREE,
        name="pack",
    )(*views, *after)


def column_kernel(lo, units, ahead, in_ref, *refs):
    out_ref, held, result, bias, in_sems, out_sems = refs[-6:]
    count, lanes = held.shape[2], held.shape[4]
    length = count * PIECE
    block = bias.shape[0]

    def arrival(u, t):
        rows = pl.ds(ahead + ((lo + u) * 3 + t) * PIECE, PIECE)
        return pltpu.make_async_copy(in_ref.at[:, rows], held.at[u, t], in_sems.at[u, t])

    def departure(u):
        rows = pl.ds((lo + u) * PIECE, PIECE)
        return pltpu.make_async_copy(result.at[u], out_ref.at[:, rows], out_sems.at[u])

    for u in range(units):
        for t in range(3):
            arrival(u, t).start()
    query = lax.broadcasted_iota(jnp.int32, bias.shape, 0)
    key = lax.broadcasted_iota(jnp.int32, bias.shape, 1)
    bias[...] = jnp.where((query & (TILE - 1)) == (key & (TILE - 1)), 0.0, OFF)
    for u in range(units):
        for t in range(3):
            arrival(u, t).wait()
        for h in range(lanes // HD):
            head = slice(h * HD, h * HD + HD)
            k = held[u, 1, :, :, head].reshape(length, HD)
            v = held[u, 2, :, :, head].reshape(length, HD)
            for s in range(0, count, block // PIECE):
                part = slice(s, s + block // PIECE)
                q = held[u, 0, part, :, head].reshape(block, HD)
                out = softmax_sum(scores(q, k) + bias[...], v)
                result[u, part, :, head] = out.reshape(block // PIECE, PIECE, HD)
        departure(u).start()
    for u in range(units):
        departure(u).wait()


def column_attention(got, ahead, lo, units, into, after=()):
    count, _, lanes = got.shape
    length = count * PIECE
    block = min(length, 256)
    held = () if into is None else (into,)
    shape = (count, units * PIECE, lanes) if into is None else into.shape
    return pl.pallas_call(
        functools.partial(column_kernel, lo, units, ahead),
        in_specs=[ANY] * (1 + len(held) + len(after)),
        out_specs=ANY,
        out_shape=jax.ShapeDtypeStruct(shape, jnp.bfloat16),
        input_output_aliases={1: 0} if held else {},
        scratch_shapes=[
            pltpu.VMEM((units, 3, count, PIECE, lanes), jnp.bfloat16),
            pltpu.VMEM((units, count, PIECE, lanes), jnp.bfloat16),
            pltpu.VMEM((block, length), jnp.float32),
            pltpu.SemaphoreType.DMA((units, 3)),
            pltpu.SemaphoreType.DMA((units,)),
        ],
        compiler_params=pltpu.CompilerParams(vmem_limit_bytes=52 * MIB),
        cost_estimate=FREE,
        name="column_attention",
    )(got, *held, *after)


def stream(step, w_ref, held, sems, start=0):
    width = held.shape[2]

    def block(n):
        columns = pl.ds(start + n * width, width)
        return pltpu.make_async_copy(w_ref.at[:, columns], held.at[n], sems.at[n])

    @pl.when(step == 0)
    def _():
        for n in range(held.shape[0]):
            block(n).start()

    for n in range(held.shape[0]):

        @pl.when(step == n)
        def _():
            block(n).wait()


def stream_scratch(depth, width, step):
    return [
        pltpu.VMEM((width // step, depth, step), jnp.bfloat16),
        pltpu.SemaphoreType.DMA((width // step,)),
    ]


def project_kernel(units, begin, mine_ref, w_ref, local_ref, in_ref, *refs):
    keep_ref, send_ref, rows_ref, sum_ref, held, sems = refs[-6:]
    stream(pl.program_id(0), w_ref, held, sems, begin)

    @pl.when(pl.program_id(0) == 0)
    def _():
        count, _, lanes = in_ref.shape
        planes = count // PLANE
        columns = planes * TILE
        chunk = units * columns
        for u in range(units):
            for p in range(PLANE):
                pieces = [
                    in_ref[z * PLANE + p, u * PIECE : (u + 1) * PIECE].astype(jnp.float32)
                    for z in range(planes)
                ]
                for j in range(PIECE // TILE):
                    part = jnp.concatenate([x[j * TILE : (j + 1) * TILE] for x in pieces])
                    row = j * chunk + u * columns
                    lane = slice(p * lanes, (p + 1) * lanes)
                    rows_ref[row : row + columns, lane] = part.astype(jnp.bfloat16)

    w = held[pl.program_id(0)]
    total = jnp.dot(rows_ref[...], w, preferred_element_type=jnp.float32)
    sum_ref[...] = total.reshape(sum_ref.shape) + local_ref[...]
    mine = mine_ref[0]
    keep_ref[...] = sum_ref[mine]
    send_ref[...] = sum_ref[1 - mine].astype(jnp.bfloat16)


def project(mine, got, w, local, first, units, chunk, part, parts, after=()):
    depth = w.shape[0]
    width = w.shape[1] // parts
    count, _, lanes = got.shape
    per_column = local.shape[0]
    step = 1024
    steps = width // step
    return pl.pallas_call(
        functools.partial(project_kernel, units, part * width),
        grid=(width // step,),
        in_specs=[
            SMEM,
            ANY,
            pl.BlockSpec((per_column, chunk, step), lambda n: (0, first // chunk, part * steps + n)),
            pl.BlockSpec((count, units * PIECE, lanes), lambda n: (0, 0, 0)),
        ]
        + [ANY] * len(after),
        out_specs=[pl.BlockSpec((chunk, step), lambda n: (0, n))] * 2,
        out_shape=[
            jax.ShapeDtypeStruct((chunk, width), jnp.float32),
            jax.ShapeDtypeStruct((chunk, width), jnp.bfloat16),
        ],
        scratch_shapes=[
            pltpu.VMEM((2 * chunk, depth), jnp.bfloat16),
            pltpu.VMEM((2, chunk, step), jnp.float32),
            *stream_scratch(depth, width, step),
        ],
        compiler_params=pltpu.CompilerParams(vmem_limit_bytes=58 * MIB),
        cost_estimate=FREE,
        name="project",
    )(mine, w, local, got, *after)


def local_kernel(a_ref, w_ref, *refs):
    out_ref, held, sems = refs[-3:]
    stream(pl.program_id(0), w_ref, held, sems)
    w = held[pl.program_id(0)]
    out_ref[...] = jnp.dot(a_ref[...], w, preferred_element_type=jnp.float32)


def project_local(a, w, after=()):
    rows, depth = a.shape
    width = w.shape[1]
    step = 1024
    return pl.pallas_call(
        local_kernel,
        grid=(width // step,),
        in_specs=[
            pl.BlockSpec((rows, depth), lambda n: (0, 0)),
            ANY,
        ]
        + [ANY] * len(after),
        out_specs=pl.BlockSpec((rows, step), lambda n: (0, n)),
        out_shape=jax.ShapeDtypeStruct((rows, width), jnp.float32),
        scratch_shapes=stream_scratch(depth, width, step),
        compiler_params=pltpu.CompilerParams(vmem_limit_bytes=60 * MIB),
        cost_estimate=FREE,
        name="project_local",
    )(a, w, *after)


def column_chunks(planes):
    units = STRIDE // (planes * TILE)
    if units == 8:
        return ROUNDS
    return ((0, units),)


def body(
    q_local, k_local, nearby_band_contents, q_stride, k_stride, v_stride, w_local, dilated_combiner
):
    rows, width = q_stride.shape
    per_column = rows // STRIDE
    count = lax.axis_size("seq")
    planes = count // PLANE
    place = jnp.stack([lax.axis_index("seq"), jnp.int32(count)]).astype(jnp.int32)
    mine = lax.axis_index("head").astype(jnp.int32).reshape(1)
    chunks = column_chunks(planes)
    last = len(chunks) - 1

    def exchange(a):
        return lax.all_to_all(a, "seq", split_axis=0, concat_axis=0, tiled=True)

    stride = (q_stride, k_stride, v_stride)
    ahead = [0] + [PIECE * units for _, units in chunks[:-1]]
    packed, token = [], ()
    for i, (first, units) in enumerate(chunks):
        packed.append(pack(stride, first, units, ahead[i], planes, token))
        if i == 0:
            k_low, k_high, v_low, v_high = ends(k_local, nearby_band_contents, tuple(packed))
            token = (k_low,)
    packed.append(None)
    halos = direct(k_low, k_high) + direct(v_low, v_high)

    results, after = [], halos
    got = exchange(packed[0])
    for i, (first, units) in enumerate(chunks):
        if i == min(1, last):
            attn_local = band_attention(
                place, q_local, k_local, nearby_band_contents, halos, after
            )
            part_local = project_local(attn_local, w_local, (attn_local,))
            part_local = part_local.reshape(per_column, STRIDE, -1)
            after = (part_local,)
        if i == 0 and i < last:
            outs = column_attention(got, ahead[i], 0, units, packed[i + 1])
            outs = tie(outs, *after)
        else:
            outs = column_attention(got, ahead[i], 0, units, packed[i + 1], after)
        after = (outs,)
        back, got = got, exchange(outs)
        for j in range(i - 1, i + (i == last)):
            if j < 0:
                continue
            start, size = chunks[j]
            parts = 2 if j == last else 1
            for part in range(parts):
                keep, send = project(
                    mine,
                    back if j < i else got,
                    dilated_combiner,
                    part_local,
                    start,
                    size,
                    size * planes * TILE,
                    part,
                    parts,
                    after,
                )
                after = (send,)
                results.append((keep, swap(send, "head", 1), start, part, parts))
    out = None
    for keep, other, start, part, parts in results:
        out = add_into(out, keep, other, start, part, parts, rows // 2, after if out is None else ())
    return out


def solution(mesh):
    in_specs = (
        P("seq", "head"),
        P("seq", "head"),
        P("seq", "head"),
        P("seq", "head"),
        P("seq", "head"),
        P("seq", "head"),
        P("head", None),
        P("head", None),
    )
    out_specs = P(("seq", "head"), None)
    return jax.shard_map(body, mesh=mesh, in_specs=in_specs, out_specs=out_specs, check_vma=False)
```

```python
import functools

import jax
import jax.numpy as jnp
from jax import lax
from jax.experimental import pallas as pl
from jax.experimental.pallas import tpu as pltpu
from jax.sharding import PartitionSpec as P

HD = 128
STRIDE = 256
BAND = 256
PLANE = 4
TILE = 8
PIECE = 16
ROUNDS = ((0, 4), (128, 2), (192, 2))
OFF = -1e30
SCALE = HD**-0.5
LOG2E = 1.4426950408889634
MIB = 1 << 20
FREE = pl.CostEstimate(flops=0, bytes_accessed=0, transcendentals=0)

VMEM = pl.BlockSpec(memory_space=pltpu.VMEM)
SMEM = pl.BlockSpec(memory_space=pltpu.SMEM)
ANY = pl.BlockSpec(memory_space=pl.ANY)


def swap(array, axis, mask):
    count = lax.axis_size(axis)
    return lax.ppermute(array, axis, [(i, i ^ mask) for i in range(count)])


def scores(q, k):
    return lax.dot_general(q, k, (((1,), (1,)), ((), ())), preferred_element_type=jnp.float32)


def softmax_sum(score, v):
    top = jnp.max(score, axis=-1, keepdims=True)
    weight = jnp.exp2((score - top) * (SCALE * LOG2E))
    total = jnp.sum(weight, axis=-1, keepdims=True)
    out = jnp.dot(weight.astype(jnp.bfloat16), v, preferred_element_type=jnp.float32)
    return (out / total).astype(jnp.bfloat16)


def band_kernel(place_ref, q_ref, k_ref, v_ref, k_low, k_high, v_low, v_high, *refs):
    out_ref, k_all, v_all, bias = refs[-4:]
    rows = q_ref.shape[0]
    step = BAND
    blocks = rows // step

    @pl.when(pl.program_id(0) == 0)
    def _():
        query = lax.broadcasted_iota(jnp.int32, (step, BAND), 0)
        key = lax.broadcasted_iota(jnp.int32, (step, BAND), 1)
        for b in range(blocks):
            before = key >= query
            after = key <= query
            if b == 0:
                before = before & (place_ref[0] > 0)
            if b == blocks - 1:
                after = after & (place_ref[0] < place_ref[1] - 1)
            bias[b, 0] = jnp.where(before, 0.0, OFF)
            bias[b, 1] = jnp.where(after, 0.0, OFF)

    for held, low, own, high in (
        (k_all, k_low, k_ref, k_high),
        (v_all, v_low, v_ref, v_high),
    ):
        held[:BAND] = low[...]
        held[BAND : BAND + rows] = own[...]
        held[BAND + rows :] = high[...]
    for b in range(blocks):
        at = slice(b * step, b * step + step)
        near = slice(b * step, b * step + 3 * BAND)
        score = scores(q_ref[at], k_all[near])
        score = jnp.concatenate(
            [
                score[:, :BAND] + bias[b, 0],
                score[:, BAND : 2 * BAND],
                score[:, 2 * BAND :] + bias[b, 1],
            ],
            axis=1,
        )
        out_ref[at] = softmax_sum(score, v_all[near])


def band_attention(place, q, k, v, halos, after=()):
    rows, width = q.shape
    own = pl.BlockSpec((rows, HD), lambda h: (0, h))
    side = pl.BlockSpec((BAND, HD), lambda h: (0, h))
    return pl.pallas_call(
        band_kernel,
        grid=(width // HD,),
        in_specs=[SMEM, own, own, own, side, side, side, side] + [ANY] * len(after),
        out_specs=own,
        out_shape=jax.ShapeDtypeStruct(q.shape, q.dtype),
        scratch_shapes=[
            pltpu.VMEM((rows + 2 * BAND, HD), jnp.bfloat16),
            pltpu.VMEM((rows + 2 * BAND, HD), jnp.bfloat16),
            pltpu.VMEM((rows // BAND, 2, BAND, BAND), jnp.float32),
        ],
        compiler_params=pltpu.CompilerParams(vmem_limit_bytes=60 * MIB),
        cost_estimate=FREE,
        name="band_attention",
    )(place, q, k, v, *halos, *after)


def tie_kernel(*refs):
    pass


def tie(array, *after):
    return pl.pallas_call(
        tie_kernel,
        in_specs=[ANY] * (1 + len(after)),
        out_specs=ANY,
        out_shape=jax.ShapeDtypeStruct(array.shape, array.dtype),
        input_output_aliases={0: 0},
        compiler_params=pltpu.CompilerParams(vmem_limit_bytes=52 * MIB),
        cost_estimate=FREE,
        name="tie",
    )(array, *after)


def add_kernel(keep_ref, got_ref, *refs):
    refs[-1][...] = (keep_ref[...] + got_ref[...].astype(jnp.float32)).astype(jnp.bfloat16)


def add_into(out, keep, got, first, part, parts, rows, after=()):
    chunk, width = keep.shape
    step = width
    spec = pl.BlockSpec((chunk, step), lambda n: (0, n))
    held = () if out is None else (out,)
    return pl.pallas_call(
        add_kernel,
        grid=(width // step,),
        in_specs=[spec, spec] + [ANY] * (len(held) + len(after)),
        out_specs=pl.BlockSpec((chunk, step), lambda n: (first // chunk, part)),
        out_shape=jax.ShapeDtypeStruct((rows, parts * width), jnp.bfloat16),
        input_output_aliases={2: 0} if held else {},
        compiler_params=pltpu.CompilerParams(vmem_limit_bytes=16 * MIB),
        cost_estimate=FREE,
        name="add_into",
    )(keep, got, *held, *after)


def ends_kernel(in_ref, *refs):
    low, high = refs[-2:]
    low[...] = in_ref[in_ref.shape[0] - BAND :]
    high[...] = in_ref[:BAND]


def ends(array, after=()):
    shape = jax.ShapeDtypeStruct((BAND, array.shape[1]), array.dtype)
    return pl.pallas_call(
        ends_kernel,
        grid=(1,),
        in_specs=[pl.BlockSpec(array.shape, lambda n: (0, 0))] + [ANY] * len(after),
        out_specs=[pl.BlockSpec(shape.shape, lambda n: (0, 0))] * 2,
        out_shape=[shape] * 2,
        compiler_params=pltpu.CompilerParams(vmem_limit_bytes=60 * MIB),
        cost_estimate=FREE,
        name="ends",
    )(array, *after)


def direct(low, high):
    count = lax.axis_size("seq")
    return (
        lax.ppermute(low, "seq", [(i, i + 1) for i in range(count - 1)]),
        lax.ppermute(high, "seq", [(i + 1, i) for i in range(count - 1)]),
    )


def pack_kernel(planes, ahead, q_ref, k_ref, v_ref, *refs):
    out_ref = refs[-1]
    lanes = out_ref.shape[-1]
    per_column, columns, _ = q_ref.shape
    many = columns // (planes * TILE)
    for i, t in [(i, t) for i in range(many) for t in range(3)]:
        held = (q_ref, k_ref, v_ref)[t]
        unit = pl.program_id(0) * many + i
        group = slice(i * planes * TILE, (i + 1) * planes * TILE)
        rows = [held[j, group].astype(jnp.float32) for j in range(per_column)]
        at = pl.ds(pl.multiple_of(ahead + (unit * 3 + t) * PIECE, PIECE), PIECE)
        for z in range(planes):
            piece = jnp.concatenate([r[z * TILE : (z + 1) * TILE] for r in rows])
            piece = piece.astype(jnp.bfloat16)
            for p in range(PLANE):
                out_ref[z * PLANE + p, at] = piece[:, p * lanes : (p + 1) * lanes]


def pack(arrays, first, units, ahead, planes, after=()):
    rows, width = arrays[0].shape
    per_column = rows // STRIDE
    lanes = width // PLANE
    columns = 2 * planes * TILE
    views = [a.reshape(per_column, STRIDE, width) for a in arrays]
    spec = pl.BlockSpec((per_column, columns, width), lambda n: (0, first // columns + n, 0))
    shape = (planes * PLANE, ahead + 3 * PIECE * units, lanes)
    return pl.pallas_call(
        functools.partial(pack_kernel, planes, ahead),
        grid=(units // 2,),
        in_specs=[spec] * 3 + [ANY] * len(after),
        out_specs=pl.BlockSpec(shape, lambda n: (0, 0, 0)),
        out_shape=jax.ShapeDtypeStruct(shape, jnp.bfloat16),
        compiler_params=pltpu.CompilerParams(vmem_limit_bytes=60 * MIB),
        cost_estimate=FREE,
        name="pack",
    )(*views, *after)


def column_kernel(lo, units, ahead, in_ref, *refs):
    out_ref, held, result, bias, in_sems, out_sems = refs[-6:]
    count, lanes = held.shape[2], held.shape[4]
    length = count * PIECE
    block = bias.shape[0]

    def arrival(u, t):
        rows = pl.ds(ahead + ((lo + u) * 3 + t) * PIECE, PIECE)
        return pltpu.make_async_copy(in_ref.at[:, rows], held.at[u, t], in_sems.at[u, t])

    def departure(u):
        rows = pl.ds((lo + u) * PIECE, PIECE)
        return pltpu.make_async_copy(result.at[u], out_ref.at[:, rows], out_sems.at[u])

    for u in range(units):
        for t in range(3):
            arrival(u, t).start()
    query = lax.broadcasted_iota(jnp.int32, bias.shape, 0)
    key = lax.broadcasted_iota(jnp.int32, bias.shape, 1)
    bias[...] = jnp.where((query & (TILE - 1)) == (key & (TILE - 1)), 0.0, OFF)
    for u in range(units):
        for t in range(3):
            arrival(u, t).wait()
        for h in range(lanes // HD):
            head = slice(h * HD, h * HD + HD)
            k = held[u, 1, :, :, head].reshape(length, HD)
            v = held[u, 2, :, :, head].reshape(length, HD)
            for s in range(0, count, block // PIECE):
                part = slice(s, s + block // PIECE)
                q = held[u, 0, part, :, head].reshape(block, HD)
                out = softmax_sum(scores(q, k) + bias[...], v)
                result[u, part, :, head] = out.reshape(block // PIECE, PIECE, HD)
        departure(u).start()
    for u in range(units):
        departure(u).wait()


def column_attention(got, ahead, lo, units, into, after=()):
    count, _, lanes = got.shape
    length = count * PIECE
    block = min(length, 256)
    held = () if into is None else (into,)
    shape = (count, units * PIECE, lanes) if into is None else into.shape
    return pl.pallas_call(
        functools.partial(column_kernel, lo, units, ahead),
        in_specs=[ANY] * (1 + len(held) + len(after)),
        out_specs=ANY,
        out_shape=jax.ShapeDtypeStruct(shape, jnp.bfloat16),
        input_output_aliases={1: 0} if held else {},
        scratch_shapes=[
            pltpu.VMEM((units, 3, count, PIECE, lanes), jnp.bfloat16),
            pltpu.VMEM((units, count, PIECE, lanes), jnp.bfloat16),
            pltpu.VMEM((block, length), jnp.float32),
            pltpu.SemaphoreType.DMA((units, 3)),
            pltpu.SemaphoreType.DMA((units,)),
        ],
        compiler_params=pltpu.CompilerParams(vmem_limit_bytes=52 * MIB),
        cost_estimate=FREE,
        name="column_attention",
    )(got, *held, *after)


def stream(step, w_ref, held, sems, start=0):
    width = held.shape[2]

    def block(n):
        columns = pl.ds(start + n * width, width)
        return pltpu.make_async_copy(w_ref.at[:, columns], held.at[n], sems.at[n])

    @pl.when(step == 0)
    def _():
        for n in range(held.shape[0]):
            block(n).start()

    for n in range(held.shape[0]):

        @pl.when(step == n)
        def _():
            block(n).wait()


def stream_scratch(depth, width, step):
    return [
        pltpu.VMEM((width // step, depth, step), jnp.bfloat16),
        pltpu.SemaphoreType.DMA((width // step,)),
    ]


def project_kernel(units, begin, mine_ref, w_ref, local_ref, in_ref, *refs):
    keep_ref, send_ref, rows_ref, sum_ref, held, sems = refs[-6:]
    stream(pl.program_id(0), w_ref, held, sems, begin)

    @pl.when(pl.program_id(0) == 0)
    def _():
        count, _, lanes = in_ref.shape
        planes = count // PLANE
        columns = planes * TILE
        chunk = units * columns
        for u in range(units):
            for p in range(PLANE):
                pieces = [
                    in_ref[z * PLANE + p, u * PIECE : (u + 1) * PIECE].astype(jnp.float32)
                    for z in range(planes)
                ]
                for j in range(PIECE // TILE):
                    part = jnp.concatenate([x[j * TILE : (j + 1) * TILE] for x in pieces])
                    row = j * chunk + u * columns
                    lane = slice(p * lanes, (p + 1) * lanes)
                    rows_ref[row : row + columns, lane] = part.astype(jnp.bfloat16)

    w = held[pl.program_id(0)]
    total = jnp.dot(rows_ref[...], w, preferred_element_type=jnp.float32)
    sum_ref[...] = total.reshape(sum_ref.shape) + local_ref[...]
    mine = mine_ref[0]
    keep_ref[...] = sum_ref[mine]
    send_ref[...] = sum_ref[1 - mine].astype(jnp.bfloat16)


def project(mine, got, w, local, first, units, chunk, part, parts, after=()):
    depth = w.shape[0]
    width = w.shape[1] // parts
    count, _, lanes = got.shape
    per_column = local.shape[0]
    step = 1024
    steps = width // step
    return pl.pallas_call(
        functools.partial(project_kernel, units, part * width),
        grid=(width // step,),
        in_specs=[
            SMEM,
            ANY,
            pl.BlockSpec((per_column, chunk, step), lambda n: (0, first // chunk, part * steps + n)),
            pl.BlockSpec((count, units * PIECE, lanes), lambda n: (0, 0, 0)),
        ]
        + [ANY] * len(after),
        out_specs=[pl.BlockSpec((chunk, step), lambda n: (0, n))] * 2,
        out_shape=[
            jax.ShapeDtypeStruct((chunk, width), jnp.float32),
            jax.ShapeDtypeStruct((chunk, width), jnp.bfloat16),
        ],
        scratch_shapes=[
            pltpu.VMEM((2 * chunk, depth), jnp.bfloat16),
            pltpu.VMEM((2, chunk, step), jnp.float32),
            *stream_scratch(depth, width, step),
        ],
        compiler_params=pltpu.CompilerParams(vmem_limit_bytes=58 * MIB),
        cost_estimate=FREE,
        name="project",
    )(mine, w, local, got, *after)


def local_kernel(a_ref, w_ref, *refs):
    out_ref, held, sems = refs[-3:]
    stream(pl.program_id(0), w_ref, held, sems)
    w = held[pl.program_id(0)]
    out_ref[...] = jnp.dot(a_ref[...], w, preferred_element_type=jnp.float32)


def project_local(a, w, after=()):
    rows, depth = a.shape
    width = w.shape[1]
    step = 1024
    return pl.pallas_call(
        local_kernel,
        grid=(width // step,),
        in_specs=[
            pl.BlockSpec((rows, depth), lambda n: (0, 0)),
            ANY,
        ]
        + [ANY] * len(after),
        out_specs=pl.BlockSpec((rows, step), lambda n: (0, n)),
        out_shape=jax.ShapeDtypeStruct((rows, width), jnp.float32),
        scratch_shapes=stream_scratch(depth, width, step),
        compiler_params=pltpu.CompilerParams(vmem_limit_bytes=60 * MIB),
        cost_estimate=FREE,
        name="project_local",
    )(a, w, *after)


def column_chunks(planes):
    units = STRIDE // (planes * TILE)
    if units == 8:
        return ROUNDS
    return ((0, units),)


def body(
    q_local, k_local, nearby_band_contents, q_stride, k_stride, v_stride, w_local, dilated_combiner
):
    rows, width = q_stride.shape
    per_column = rows // STRIDE
    count = lax.axis_size("seq")
    planes = count // PLANE
    place = jnp.stack([lax.axis_index("seq"), jnp.int32(count)]).astype(jnp.int32)
    mine = lax.axis_index("head").astype(jnp.int32).reshape(1)
    chunks = column_chunks(planes)
    last = len(chunks) - 1

    def exchange(a):
        return lax.all_to_all(a, "seq", split_axis=0, concat_axis=0, tiled=True)

    stride = (q_stride, k_stride, v_stride)
    ahead = [0] + [PIECE * units for _, units in chunks[:-1]]
    packed, token = [], ()
    for i, (first, units) in enumerate(chunks):
        packed.append(pack(stride, first, units, ahead[i], planes, token))
        if i == 0:
            k_low, k_high = ends(k_local, tuple(packed))
            v_low, v_high = ends(nearby_band_contents, (k_low,))
            token = (v_low,)
    packed.append(None)
    halos = direct(k_low, k_high) + direct(v_low, v_high)

    results, after = [], halos
    got = exchange(packed[0])
    for i, (first, units) in enumerate(chunks):
        if i == min(1, last):
            attn_local = band_attention(
                place, q_local, k_local, nearby_band_contents, halos, after
            )
            part_local = project_local(attn_local, w_local, (attn_local,))
            part_local = part_local.reshape(per_column, STRIDE, -1)
            after = (part_local,)
        if i == 0 and i < last:
            outs = column_attention(got, ahead[i], 0, units, packed[i + 1])
            outs = tie(outs, *after)
        else:
            outs = column_attention(got, ahead[i], 0, units, packed[i + 1], after)
        after = (outs,)
        back, got = got, exchange(outs)
        for j in range(i - 1, i + (i == last)):
            if j < 0:
                continue
            start, size = chunks[j]
            parts = 2 if j >= last - 1 else 1
            for part in range(parts):
                keep, send = project(
                    mine,
                    back if j < i else got,
                    dilated_combiner,
                    part_local,
                    start,
                    size,
                    size * planes * TILE,
                    part,
                    parts,
                    after,
                )
                after = (send,)
                results.append((keep, swap(send, "head", 1), start, part, parts))
    out = None
    for keep, other, start, part, parts in results:
        out = add_into(out, keep, other, start, part, parts, rows // 2, after if out is None else ())
    return out


def solution(mesh):
    in_specs = (
        P("seq", "head"),
        P("seq", "head"),
        P("seq", "head"),
        P("seq", "head"),
        P("seq", "head"),
        P("seq", "head"),
        P("head", None),
        P("head", None),
    )
    out_specs = P(("seq", "head"), None)
    return jax.shard_map(body, mesh=mesh, in_specs=in_specs, out_specs=out_specs, check_vma=False)
```

```python
import functools

import jax
import jax.numpy as jnp
from jax import lax
from jax.experimental import pallas as pl
from jax.experimental.pallas import tpu as pltpu
from jax.sharding import PartitionSpec as P

HD = 128
STRIDE = 256
BAND = 256
PLANE = 4
TILE = 8
PIECE = 16
BLOCK = 512
ROUNDS = ((0, 4), (128, 2), (192, 2))
OFF = -1e30
SCALE = HD**-0.5
LOG2E = 1.4426950408889634
MIB = 1 << 20
FREE = pl.CostEstimate(flops=0, bytes_accessed=0, transcendentals=0)

VMEM = pl.BlockSpec(memory_space=pltpu.VMEM)
SMEM = pl.BlockSpec(memory_space=pltpu.SMEM)
ANY = pl.BlockSpec(memory_space=pl.ANY)


def swap(array, axis, mask):
    count = lax.axis_size(axis)
    return lax.ppermute(array, axis, [(i, i ^ mask) for i in range(count)])


def scores(q, k):
    return lax.dot_general(q, k, (((1,), (1,)), ((), ())), preferred_element_type=jnp.float32)


def softmax_sum(score, v):
    top = jnp.max(score, axis=-1, keepdims=True)
    weight = jnp.exp2((score - top) * (SCALE * LOG2E))
    total = jnp.sum(weight, axis=-1, keepdims=True)
    out = jnp.dot(weight.astype(jnp.bfloat16), v, preferred_element_type=jnp.float32)
    return (out / total).astype(jnp.bfloat16)


def band_kernel(place_ref, q_ref, k_ref, v_ref, k_low, k_high, v_low, v_high, *refs):
    out_ref, k_all, v_all, bias = refs[-4:]
    rows = q_ref.shape[0]
    step = BAND
    blocks = rows // step

    @pl.when(pl.program_id(0) == 0)
    def _():
        query = lax.broadcasted_iota(jnp.int32, (step, BAND), 0)
        key = lax.broadcasted_iota(jnp.int32, (step, BAND), 1)
        for b in range(blocks):
            before = key >= query
            after = key <= query
            if b == 0:
                before = before & (place_ref[0] > 0)
            if b == blocks - 1:
                after = after & (place_ref[0] < place_ref[1] - 1)
            bias[b, 0] = jnp.where(before, 0.0, OFF)
            bias[b, 1] = jnp.where(after, 0.0, OFF)

    for held, low, own, high in (
        (k_all, k_low, k_ref, k_high),
        (v_all, v_low, v_ref, v_high),
    ):
        held[:BAND] = low[...]
        held[BAND : BAND + rows] = own[...]
        held[BAND + rows :] = high[...]
    for b in range(blocks):
        at = slice(b * step, b * step + step)
        near = slice(b * step, b * step + 3 * BAND)
        score = scores(q_ref[at], k_all[near])
        score = jnp.concatenate(
            [
                score[:, :BAND] + bias[b, 0],
                score[:, BAND : 2 * BAND],
                score[:, 2 * BAND :] + bias[b, 1],
            ],
            axis=1,
        )
        out_ref[at] = softmax_sum(score, v_all[near])


def band_attention(place, q, k, v, halos, after=()):
    rows, width = q.shape
    own = pl.BlockSpec((rows, HD), lambda h: (0, h))
    side = pl.BlockSpec((BAND, HD), lambda h: (0, h))
    return pl.pallas_call(
        band_kernel,
        grid=(width // HD,),
        in_specs=[SMEM, own, own, own, side, side, side, side] + [ANY] * len(after),
        out_specs=own,
        out_shape=jax.ShapeDtypeStruct(q.shape, q.dtype),
        scratch_shapes=[
            pltpu.VMEM((rows + 2 * BAND, HD), jnp.bfloat16),
            pltpu.VMEM((rows + 2 * BAND, HD), jnp.bfloat16),
            pltpu.VMEM((rows // BAND, 2, BAND, BAND), jnp.float32),
        ],
        compiler_params=pltpu.CompilerParams(vmem_limit_bytes=60 * MIB),
        cost_estimate=FREE,
        name="band_attention",
    )(place, q, k, v, *halos, *after)


def tie_kernel(*refs):
    pass


def tie(array, *after):
    return pl.pallas_call(
        tie_kernel,
        in_specs=[ANY] * (1 + len(after)),
        out_specs=ANY,
        out_shape=jax.ShapeDtypeStruct(array.shape, array.dtype),
        input_output_aliases={0: 0},
        compiler_params=pltpu.CompilerParams(vmem_limit_bytes=52 * MIB),
        cost_estimate=FREE,
        name="tie",
    )(array, *after)


def add_kernel(keep_ref, got_ref, *refs):
    refs[-1][...] = (keep_ref[...] + got_ref[...].astype(jnp.float32)).astype(jnp.bfloat16)


def add_into(out, keep, got, first, part, parts, rows, after=()):
    chunk, width = keep.shape
    step = width
    spec = pl.BlockSpec((chunk, step), lambda n: (0, n))
    held = () if out is None else (out,)
    return pl.pallas_call(
        add_kernel,
        grid=(width // step,),
        in_specs=[spec, spec] + [ANY] * (len(held) + len(after)),
        out_specs=pl.BlockSpec((chunk, step), lambda n: (first // chunk, part)),
        out_shape=jax.ShapeDtypeStruct((rows, parts * width), jnp.bfloat16),
        input_output_aliases={2: 0} if held else {},
        compiler_params=pltpu.CompilerParams(vmem_limit_bytes=16 * MIB),
        cost_estimate=FREE,
        name="add_into",
    )(keep, got, *held, *after)


def ends_kernel(in_ref, *refs):
    low, high = refs[-2:]
    low[...] = in_ref[in_ref.shape[0] - BAND :]
    high[...] = in_ref[:BAND]


def ends(array, after=()):
    shape = jax.ShapeDtypeStruct((BAND, array.shape[1]), array.dtype)
    return pl.pallas_call(
        ends_kernel,
        grid=(1,),
        in_specs=[pl.BlockSpec(array.shape, lambda n: (0, 0))] + [ANY] * len(after),
        out_specs=[pl.BlockSpec(shape.shape, lambda n: (0, 0))] * 2,
        out_shape=[shape] * 2,
        compiler_params=pltpu.CompilerParams(vmem_limit_bytes=60 * MIB),
        cost_estimate=FREE,
        name="ends",
    )(array, *after)


def direct(low, high):
    count = lax.axis_size("seq")
    return (
        lax.ppermute(low, "seq", [(i, i + 1) for i in range(count - 1)]),
        lax.ppermute(high, "seq", [(i + 1, i) for i in range(count - 1)]),
    )


def pack_kernel(planes, ahead, q_ref, k_ref, v_ref, *refs):
    out_ref = refs[-1]
    lanes = out_ref.shape[-1]
    per_column, columns, _ = q_ref.shape
    many = columns // (planes * TILE)
    for i, t in [(i, t) for i in range(many) for t in range(3)]:
        held = (q_ref, k_ref, v_ref)[t]
        unit = pl.program_id(0) * many + i
        group = slice(i * planes * TILE, (i + 1) * planes * TILE)
        rows = [held[j, group].astype(jnp.float32) for j in range(per_column)]
        at = pl.ds(pl.multiple_of(ahead + (unit * 3 + t) * PIECE, PIECE), PIECE)
        for z in range(planes):
            piece = jnp.concatenate([r[z * TILE : (z + 1) * TILE] for r in rows])
            piece = piece.astype(jnp.bfloat16)
            for p in range(PLANE):
                out_ref[z * PLANE + p, at] = piece[:, p * lanes : (p + 1) * lanes]


def pack(arrays, first, units, ahead, planes, after=()):
    rows, width = arrays[0].shape
    per_column = rows // STRIDE
    lanes = width // PLANE
    columns = 2 * planes * TILE
    views = [a.reshape(per_column, STRIDE, width) for a in arrays]
    spec = pl.BlockSpec((per_column, columns, width), lambda n: (0, first // columns + n, 0))
    shape = (planes * PLANE, ahead + 3 * PIECE * units, lanes)
    return pl.pallas_call(
        functools.partial(pack_kernel, planes, ahead),
        grid=(units // 2,),
        in_specs=[spec] * 3 + [ANY] * len(after),
        out_specs=pl.BlockSpec(shape, lambda n: (0, 0, 0)),
        out_shape=jax.ShapeDtypeStruct(shape, jnp.bfloat16),
        compiler_params=pltpu.CompilerParams(vmem_limit_bytes=60 * MIB),
        cost_estimate=FREE,
        name="pack",
    )(*views, *after)


def column_kernel(lo, units, ahead, in_ref, *refs):
    out_ref, held, result, bias, in_sems, out_sems = refs[-6:]
    count, lanes = held.shape[2], held.shape[4]
    length = count * PIECE
    block = bias.shape[0]

    def arrival(u, t):
        rows = pl.ds(ahead + ((lo + u) * 3 + t) * PIECE, PIECE)
        return pltpu.make_async_copy(in_ref.at[:, rows], held.at[u, t], in_sems.at[u, t])

    def departure(u):
        rows = pl.ds((lo + u) * PIECE, PIECE)
        return pltpu.make_async_copy(result.at[u], out_ref.at[:, rows], out_sems.at[u])

    for u in range(units):
        for t in range(3):
            arrival(u, t).start()
    query = lax.broadcasted_iota(jnp.int32, bias.shape, 0)
    key = lax.broadcasted_iota(jnp.int32, bias.shape, 1)
    bias[...] = jnp.where((query & (TILE - 1)) == (key & (TILE - 1)), 0.0, OFF)
    for u in range(units):
        for t in range(3):
            arrival(u, t).wait()
        for h in range(lanes // HD):
            head = slice(h * HD, h * HD + HD)
            k = held[u, 1, :, :, head].reshape(length, HD)
            v = held[u, 2, :, :, head].reshape(length, HD)
            for s in range(0, count, block // PIECE):
                part = slice(s, s + block // PIECE)
                q = held[u, 0, part, :, head].reshape(block, HD)
                out = softmax_sum(scores(q, k) + bias[...], v)
                result[u, part, :, head] = out.reshape(block // PIECE, PIECE, HD)
        departure(u).start()
    for u in range(units):
        departure(u).wait()


def column_attention(got, ahead, lo, units, into, after=()):
    count, _, lanes = got.shape
    length = count * PIECE
    block = min(length, 256)
    held = () if into is None else (into,)
    shape = (count, units * PIECE, lanes) if into is None else into.shape
    return pl.pallas_call(
        functools.partial(column_kernel, lo, units, ahead),
        in_specs=[ANY] * (1 + len(held) + len(after)),
        out_specs=ANY,
        out_shape=jax.ShapeDtypeStruct(shape, jnp.bfloat16),
        input_output_aliases={1: 0} if held else {},
        scratch_shapes=[
            pltpu.VMEM((units, 3, count, PIECE, lanes), jnp.bfloat16),
            pltpu.VMEM((units, count, PIECE, lanes), jnp.bfloat16),
            pltpu.VMEM((block, length), jnp.float32),
            pltpu.SemaphoreType.DMA((units, 3)),
            pltpu.SemaphoreType.DMA((units,)),
        ],
        compiler_params=pltpu.CompilerParams(vmem_limit_bytes=52 * MIB),
        cost_estimate=FREE,
        name="column_attention",
    )(got, *held, *after)


def stream(step, w_ref, held, sems, start=0):
    width = held.shape[2]

    def block(n):
        columns = pl.ds(start + n * width, width)
        return pltpu.make_async_copy(w_ref.at[:, columns], held.at[n], sems.at[n])

    @pl.when(step == 0)
    def _():
        for n in range(held.shape[0]):
            block(n).start()

    for n in range(held.shape[0]):

        @pl.when(step == n)
        def _():
            block(n).wait()


def stream_scratch(depth, width, step):
    return [
        pltpu.VMEM((width // step, depth, step), jnp.bfloat16),
        pltpu.SemaphoreType.DMA((width // step,)),
    ]


def project_kernel(units, first, begin, mine_ref, w_ref, local_ref, in_ref, *refs):
    keep_ref, send_ref, rows_ref, got, local, held, keep, send, sems = refs[-9:]
    count, _, lanes = got.shape
    planes = count // PLANE
    columns = planes * TILE
    chunk = units * columns
    blocks, _, width = held.shape

    fetch = pltpu.make_async_copy(in_ref.at[:, pl.ds(0, units * PIECE)], got, sems.at[4 * blocks])
    fetch.start()

    def copies(n):
        at = pl.ds(begin + n * width, width)
        to = pl.ds(n * width, width)
        rows = pl.ds(first, chunk)
        pairs = (
            (w_ref.at[:, at], held.at[n]),
            (local_ref.at[:, rows, at], local.at[n]),
            (keep.at[n], keep_ref.at[:, to]),
            (send.at[n], send_ref.at[:, to]),
        )
        return [
            pltpu.make_async_copy(a, b, sems.at[k * blocks + n]) for k, (a, b) in enumerate(pairs)
        ]

    for n in range(blocks):
        for copy in copies(n)[:2]:
            copy.start()
    fetch.wait()
    for u in range(units):
        for p in range(PLANE):
            pieces = [
                got[z * PLANE + p, u * PIECE : (u + 1) * PIECE].astype(jnp.float32)
                for z in range(planes)
            ]
            for j in range(PIECE // TILE):
                part = jnp.concatenate([x[j * TILE : (j + 1) * TILE] for x in pieces])
                row = j * chunk + u * columns
                lane = slice(p * lanes, (p + 1) * lanes)
                rows_ref[row : row + columns, lane] = part.astype(jnp.bfloat16)
    mine = mine_ref[0]
    for n in range(blocks):
        for copy in copies(n)[:2]:
            copy.wait()
        total = jnp.dot(rows_ref[...], held[n], preferred_element_type=jnp.float32)
        low = total[:chunk] + local[n, 0]
        high = total[chunk:] + local[n, 1]
        keep[n] = jnp.where(mine == 0, low, high)
        send[n] = jnp.where(mine == 0, high, low).astype(jnp.bfloat16)
        for copy in copies(n)[2:]:
            copy.start()
    for n in range(blocks):
        for copy in copies(n)[2:]:
            copy.wait()


def project(mine, got, w, local, first, units, chunk, part, parts, after=()):
    depth = w.shape[0]
    width = w.shape[1] // parts
    count, _, lanes = got.shape
    blocks = width // BLOCK
    return pl.pallas_call(
        functools.partial(project_kernel, units, first, part * width),
        in_specs=[SMEM] + [ANY] * (3 + len(after)),
        out_specs=[ANY, ANY],
        out_shape=[
            jax.ShapeDtypeStruct((chunk, width), jnp.float32),
            jax.ShapeDtypeStruct((chunk, width), jnp.bfloat16),
        ],
        scratch_shapes=[
            pltpu.VMEM((2 * chunk, depth), jnp.bfloat16),
            pltpu.VMEM((count, units * PIECE, lanes), jnp.bfloat16),
            pltpu.VMEM((blocks, 2, chunk, BLOCK), jnp.float32),
            pltpu.VMEM((blocks, depth, BLOCK), jnp.bfloat16),
            pltpu.VMEM((blocks, chunk, BLOCK), jnp.float32),
            pltpu.VMEM((blocks, chunk, BLOCK), jnp.bfloat16),
            pltpu.SemaphoreType.DMA((4 * blocks + 1,)),
        ],
        compiler_params=pltpu.CompilerParams(vmem_limit_bytes=58 * MIB),
        cost_estimate=FREE,
        name="project",
    )(mine, w, local, got, *after)


def local_kernel(a_ref, w_ref, *refs):
    out_ref, held, sems = refs[-3:]
    stream(pl.program_id(0), w_ref, held, sems)
    w = held[pl.program_id(0)]
    out_ref[...] = jnp.dot(a_ref[...], w, preferred_element_type=jnp.float32)


def project_local(a, w, after=()):
    rows, depth = a.shape
    width = w.shape[1]
    step = 1024
    return pl.pallas_call(
        local_kernel,
        grid=(width // step,),
        in_specs=[
            pl.BlockSpec((rows, depth), lambda n: (0, 0)),
            ANY,
        ]
        + [ANY] * len(after),
        out_specs=pl.BlockSpec((rows, step), lambda n: (0, n)),
        out_shape=jax.ShapeDtypeStruct((rows, width), jnp.float32),
        scratch_shapes=stream_scratch(depth, width, step),
        compiler_params=pltpu.CompilerParams(vmem_limit_bytes=60 * MIB),
        cost_estimate=FREE,
        name="project_local",
    )(a, w, *after)


def column_chunks(planes):
    units = STRIDE // (planes * TILE)
    if units == 8:
        return ROUNDS
    return ((0, units),)


def body(
    q_local, k_local, nearby_band_contents, q_stride, k_stride, v_stride, w_local, dilated_combiner
):
    rows, width = q_stride.shape
    per_column = rows // STRIDE
    count = lax.axis_size("seq")
    planes = count // PLANE
    place = jnp.stack([lax.axis_index("seq"), jnp.int32(count)]).astype(jnp.int32)
    mine = lax.axis_index("head").astype(jnp.int32).reshape(1)
    chunks = column_chunks(planes)
    last = len(chunks) - 1

    def exchange(a):
        return lax.all_to_all(a, "seq", split_axis=0, concat_axis=0, tiled=True)

    stride = (q_stride, k_stride, v_stride)
    ahead = [0] + [PIECE * units for _, units in chunks[:-1]]
    packed, token = [], ()
    for i, (first, units) in enumerate(chunks):
        packed.append(pack(stride, first, units, ahead[i], planes, token))
        if i == 0:
            k_low, k_high = ends(k_local, tuple(packed))
            v_low, v_high = ends(nearby_band_contents, (k_low,))
            token = (v_low,)
    packed.append(None)
    halos = direct(k_low, k_high) + direct(v_low, v_high)

    results, after = [], halos
    got = exchange(packed[0])
    for i, (first, units) in enumerate(chunks):
        if i == min(1, last):
            attn_local = band_attention(
                place, q_local, k_local, nearby_band_contents, halos, after
            )
            part_local = project_local(attn_local, w_local, (attn_local,))
            part_local = part_local.reshape(per_column, STRIDE, -1)
            after = (part_local,)
        if i == 0 and i < last:
            outs = column_attention(got, ahead[i], 0, units, packed[i + 1])
            outs = tie(outs, *after)
        else:
            outs = column_attention(got, ahead[i], 0, units, packed[i + 1], after)
        after = (outs,)
        back, got = got, exchange(outs)
        for j in range(i - 1, i + (i == last)):
            if j < 0:
                continue
            start, size = chunks[j]
            parts = 2 if j >= last - 1 else 1
            for part in range(parts):
                keep, send = project(
                    mine,
                    back if j < i else got,
                    dilated_combiner,
                    part_local,
                    start,
                    size,
                    size * planes * TILE,
                    part,
                    parts,
                    after,
                )
                after = (send,)
                results.append((keep, swap(send, "head", 1), start, part, parts))
    out = None
    for keep, other, start, part, parts in results:
        out = add_into(out, keep, other, start, part, parts, rows // 2, after if out is None else ())
    return out


def solution(mesh):
    in_specs = (
        P("seq", "head"),
        P("seq", "head"),
        P("seq", "head"),
        P("seq", "head"),
        P("seq", "head"),
        P("seq", "head"),
        P("head", None),
        P("head", None),
    )
    out_specs = P(("seq", "head"), None)
    return jax.shard_map(body, mesh=mesh, in_specs=in_specs, out_specs=out_specs, check_vma=False)
```
